512 devices in a mesh: dp: 8 (over x, core), mp: 64 (over z, y).
Axes of the slice: x: 4, y: 8, z: 8, core: 2. Of those that a mesh axis runs over, the one named last changes fastest.
Arguments:
- inputs: bfloat16 [1024, 6144], P('dp', 'mp'), may hold values from -6 to 6
- gain: bfloat16 [6144], P('mp'), may hold values from 0.099609375 to 1.8984375
- w_in: bfloat16 [6144, 16384], P('dp', 'mp'), may hold values from -0.078125 to 0.078125
- w_out: bfloat16 [16384, 6144], P('mp', 'dp'), may hold values from -0.046875 to 0.046875
- targets: bfloat16 [1024, 6144], P('dp', 'mp'), may hold values from -7.5 to 7.5
Outputs:
- input_grad: bfloat16 [1024, 6144], P('dp', 'mp')
- gain_grad: float32 [6144], P('mp')
- w_in_grad: float32 [6144, 16384], P('dp', 'mp')
- w_out_grad: float32 [16384, 6144], P('mp', 'dp')
The draws below stay inside these ranges and needn't reach their ends.
All inputs are finite; a program needn't handle non-finite values.
Results may differ from the reference program's by a relative error of at most 0.0055.
Values may be sent and summed in bfloat16 or wider, within the bound.
A program may use at most 64 MiB of HBM per device.

```python
import jax
import jax.numpy as jnp
from jax import lax

D = 6144
FF = 16384
TOKENS = 1024


def draw_targets(key, part):
    key = jax.random.fold_in(key, 7)
    base_key, scale_key = jax.random.split(key, 2)
    base_draw = jnp.clip(jax.random.normal(base_key, (TOKENS, D), jnp.float32), -5.0, 5.0)
    spread = jnp.exp(jax.random.uniform(scale_key, (TOKENS, 1), jnp.float32, 0.0, 2.302585))
    ramp = 1.0 + 2.0 * jnp.arange(TOKENS, dtype=jnp.float32)[:, None] / (TOKENS - 1)
    return (0.05 * base_draw * spread * ramp).astype(jnp.bfloat16)


def steps_of(rng, shape, shards, least, largest):
    factor_of, own = 1.0, jax.random.fold_in(rng, 6)
    for dim, blocks in shards:
        heights = jnp.exp(jax.random.uniform(jax.random.fold_in(own, dim), (blocks,), jnp.float32, least / len(shards), largest / len(shards)))
        factor_of = factor_of * jnp.repeat(heights, shape[dim] // blocks).reshape([-1 if axis == dim else 1 for axis in range(len(shape))])
    return factor_of


def gaussian(stream_key, shape, deviation, most, cuts=(), kind=jnp.bfloat16):
    entries = deviation * jax.random.normal(stream_key, shape, jnp.float32)
    if cuts:
        entries = entries * steps_of(stream_key, shape, cuts, -0.22, 0.18)
    return jnp.clip(entries, -most, most).astype(kind)


def setup_inputs(seed: int = 0) -> dict:
    arg_keys = jax.random.split(jax.random.key(seed), 6)
    return {
        "inputs": gaussian(arg_keys[0], (TOKENS, D), 1.0, 6.0, ((0, 8), (1, 64))),
        "gain": jnp.clip(1.0 + 0.18 * jax.random.normal(arg_keys[1], (D,), jnp.float32), 0.099609375, 1.8984375).astype(jnp.bfloat16),
        "w_in": gaussian(arg_keys[2], (D, FF), D ** -0.5, 0.078125, ((0, 8), (1, 64))),
        "w_out": gaussian(arg_keys[3], (FF, D), FF ** -0.5, 0.046875, ((0, 64), (1, 8))),
        "targets": draw_targets(jax.random.fold_in(arg_keys[5], 71), 0),
    }


epsilon = 1e-06

def gelu_value(values):
    return 0.5 * values * (1.0 + jax.scipy.special.erf(values * 0.7071067811865476))

def gelu_slope(values):
    cumul = 0.5 * (1.0 + jax.scipy.special.erf(values * 0.7071067811865476))
    return cumul + values * jnp.exp(-0.5 * values * values) * 0.3989422804014327

def reference(inputs, gain, w_in, w_out, targets):
    raw_rows = inputs.astype(jnp.float32)
    row_mean = lax.optimization_barrier(jnp.mean(raw_rows, axis=1, keepdims=True))
    mean_square = lax.optimization_barrier(jnp.mean(raw_rows * raw_rows, axis=1, keepdims=True))
    inv_std = lax.rsqrt(mean_square - row_mean * row_mean + epsilon)
    centred = (raw_rows - row_mean) * inv_std
    gain_wide = gain.astype(jnp.float32)
    normed = (centred * gain_wide).astype(jnp.bfloat16)
    pre_act = jnp.dot(normed, w_in, preferred_element_type=jnp.float32)
    activated = gelu_value(pre_act).astype(jnp.bfloat16)
    act_grad = jnp.dot(targets, w_out.T, preferred_element_type=jnp.float32)
    pre_grad = (act_grad * gelu_slope(pre_act)).astype(jnp.bfloat16)
    norm_grad = jnp.dot(pre_grad, w_in.T, preferred_element_type=jnp.float32)
    scaled_grad = norm_grad * gain_wide
    first_mean = lax.optimization_barrier(jnp.mean(scaled_grad, axis=1, keepdims=True))
    second_mean = lax.optimization_barrier(jnp.mean(scaled_grad * centred, axis=1, keepdims=True))
    input_grad = (targets.astype(jnp.float32) + inv_std * (scaled_grad - first_mean - centred * second_mean)).astype(jnp.bfloat16)
    gain_grad = lax.optimization_barrier(jnp.sum(norm_grad * centred, axis=0))
    w_in_grad = jnp.dot(normed.T, pre_grad, preferred_element_type=jnp.float32)
    w_out_grad = jnp.dot(activated.T, targets, preferred_element_type=jnp.float32)
    return (input_grad, gain_grad, w_in_grad, w_out_grad)
```

```python
import functools

import jax
import jax.numpy as jnp
from jax import lax
from jax.experimental import pallas as pl
from jax.experimental.pallas import tpu as pltpu
from jax.sharding import PartitionSpec as P

epsilon = 1e-06
MESH = pl.DeviceIdType.MESH
bf16, f32 = jnp.bfloat16, jnp.float32
D = 6144
F = 96
K = 768
H = 256
Q = 32
HALF = F // 2


def gelu_parts(values):
    cumul = 0.5 * (1.0 + lax.erf(values * 0.7071067811865476))
    slope = cumul + values * jnp.exp(-0.5 * values * values) * 0.3989422804014327
    return values * cumul, slope


def turned(rows):
    return jnp.broadcast_to(rows, (128, 128)).T


SCRATCH = dict(
    w1=((K, H), bf16), w2=((H, K), bf16),
    pad=((2, 128, 128), f32), own=((2, F, 128), bf16), gown=((8, 128), f32),
    xg=((8, 8, F, 128), bf16), tg=((8, 8, F, 128), bf16), nt=((8, 8, F, 128), bf16),
    gg=((8, 8, 128), f32), gb=((8, F, 128), f32),
    sta=((8, 8, 128), f32), stb=((8, 8, 128), f32), stc=((8, 8, 128), f32),
    part=((2, 4, 2, Q, 1024), f32), cs=((4, 2, Q, 1024), bf16), cr=((4, 2, Q, 1024), bf16),
    xs=((3, 2, Q, 1024), bf16), xr=((3, 2, Q, 1024), bf16),
    pre=((2, Q, 1024), f32), comb=((8, 2, Q, 1024), bf16),
    u=((8, H), f32), s2p=((8, 8, 128), f32), s2r=((8, 8, 128), f32),
    s2y=((8, 8, 128), f32), s2z=((8, 8, 128), f32),
    ng=((8, 8, F, 128), f32), ra=((2, 2, 4, 8, HALF, 128), bf16), sa=((2, 2, 4, 8, HALF, 128), bf16),
    fs=((2, 8, HALF, 128), bf16), fr=((2, 8, HALF, 128), bf16),
    w1g=((K, H), f32), w2g=((H, K), f32), ge=((8, 8, 128), f32),
)
SEMS = dict(
    loc=(6,), perm=(2, 3), sx=(2, 7), stg=(2, 7), sg=(2, 7), ssa=(2, 7), ssb=(2, 7), ssc=(2, 7),
    ring=(2, 2, 2, 4, 2), core=(2, 4), xx=(2, 3), ax=(2, 3), ac=(2, 4),
    s2a=(2, 7), s2b=(2, 7), s2c=(2, 7), rs=(2, 2, 2, 4, 2), fin=(2, 2, 8), gx=(2, 7),
)


def kernel(x_ref, t_ref, g_ref, w1_hbm, w2_hbm, ig_ref, gg_out, w1g_hbm, w2g_hbm, *scratch):
    S = dict(zip(list(SCRATCH) + list(SEMS), scratch, strict=True))
    d, m = lax.axis_index("dp"), lax.axis_index("mp")
    z, y = m // 8, m % 8
    chip, core = d // 2, d % 2
    diag = d == z
    off_diag = jnp.logical_not(diag)
    sends = []

    def at(dp, zz, yy):
        return (dp, zz * 8 + yy)

    def remote(src, dst, sem, index, dev, landing=None):
        return pltpu.make_async_remote_copy(
            src_ref=src, dst_ref=dst, send_sem=S[sem].at[(0, *index)],
            recv_sem=S[sem].at[(1, *(landing or index))], device_id=dev, device_id_type=MESH)

    def go(src, dst, sem, index, dev):
        copy = remote(src, dst, sem, index, dev)
        copy.start()
        sends.append(copy)
        return copy

    def along(axis, i):
        if axis == "dp":
            return at((d + i) % 8, z, y)
        if axis == "z":
            return at(d, (z + i) % 8, y)
        return at(d, z, (y + i) % 8)

    def spread(buf, slot, sem, axis):
        return [go(S[buf].at[slot], S[buf].at[slot], sem, (i - 1,), along(axis, i)) for i in range(1, 8)]

    def arrive(copies):
        for copy in copies:
            copy.wait_recv()

    load1 = pltpu.make_async_copy(w1_hbm, S["w1"], S["loc"].at[0])
    load2 = pltpu.make_async_copy(w2_hbm, S["w2"], S["loc"].at[1])
    load1.start()
    load2.start()

    barrier = pltpu.get_barrier_semaphore()

    def hail(dev):
        pl.semaphore_signal(barrier, inc=1, device_id=dev, device_id_type=MESH)

    for axis in ("dp", "z", "y"):
        for i in range(1, 8):
            hail(along(axis, i))

    @pl.when(off_diag)
    def _():
        for i in range(1, 8):
            hail(at((d + i) % 8, d, y))
            hail(at(z, (z + i) % 8, y))
            hail(at(z, d, (y + i) % 8))

    S["pad"][...] = jnp.zeros_like(S["pad"])
    S["pad"][0, :, :F] = x_ref[...].astype(f32)
    S["pad"][1, :, :F] = t_ref[...].astype(f32)
    for i in range(2):
        S["own"][i] = S["pad"][i].T[:F].astype(bf16)
    S["gown"][...] = jnp.zeros_like(S["gown"])
    S["gown"][:, :F] = jnp.broadcast_to(g_ref[...].astype(f32), (8, F))

    @pl.when(off_diag)
    def _():
        pl.semaphore_wait(barrier, 42)

    @pl.when(diag)
    def _():
        pl.semaphore_wait(barrier, 21)

    perm = [
        (S["own"].at[0], S["xg"].at[d, y], S["xg"].at[z, y]),
        (S["own"].at[1], S["tg"].at[d, y], S["tg"].at[z, y]),
        (S["gown"], S["gg"].at[y], S["gg"].at[y]),
    ]
    perm = [remote(src, dst, "perm", (i,), at(z, d, y)) for i, (src, dst, _) in enumerate(perm)]

    @pl.when(off_diag)
    def _():
        for copy in perm:
            copy.start()

    @pl.when(diag)
    def _():
        pltpu.make_async_copy(S["own"].at[0], S["xg"].at[z, y], S["perm"].at[1, 0]).start()
        pltpu.make_async_copy(S["own"].at[1], S["tg"].at[z, y], S["perm"].at[1, 1]).start()
        pltpu.make_async_copy(S["gown"], S["gg"].at[y], S["perm"].at[1, 2]).start()

    arrive(perm)

    gx = [
        go(S["xg"].at[z, y], S["xg"].at[z, y], "sx", (i - 1,), along("z", i)) for i in range(1, 8)]
    gt = [go(S["tg"].at[z, y], S["tg"].at[z, y], "stg", (i - 1,), along("y", i)) for i in range(1, 8)]
    ggain = spread("gg", y, "sg", "y")
    piece = S["xg"][z, y].astype(f32)
    S["sta"][y] = jnp.zeros((8, 128), f32)
    S["sta"][y, 0:1] = jnp.sum(piece, axis=0, keepdims=True)
    S["sta"][y, 1:2] = jnp.sum(piece * piece, axis=0, keepdims=True)
    sta = spread("sta", y, "ssa", "y")
    arrive(gx)
    arrive(gt)

    def ring_ref(axis, origin, sub):
        half = pl.ds(4 * sub, 4)
        if axis == 0:
            return S["xg"].at[half, origin]
        return S["tg"].at[origin, half]

    ring = {}

    def ring_step(k):
        for sub in (0, 1):
            for axis in (0, 1):
                for way in (0, 1):
                    if k == 4 and sub != way:
                        continue
                    sign = 1 - 2 * way
                    me = y if axis == 0 else z
                    if k > 1:
                        ring[axis, way, k - 1, sub].wait_recv()
                    ref = ring_ref(axis, (me - sign * (k - 1) + 8) % 8, sub)
                    ring[axis, way, k, sub] = go(
                        ref, ref, "ring", (axis, way, k - 1, sub), along("yz"[axis], sign + 8))

    ring_step(1)
    arrive(sta)
    S["stb"][d] = jnp.sum(S["sta"][...], axis=0)
    stb = spread("stb", d, "ssb", "dp")
    arrive(ggain)
    load1.wait()
    load2.wait()
    total = jnp.zeros((8, H), f32)
    for i in range(8):
        rows = S["gg"][i]
        S["gb"][i] = turned(rows[0:1])[:F]
        total += jnp.dot(rows[:, :F].astype(bf16), S["w1"][F * i:F * (i + 1)], preferred_element_type=f32)
    S["u"][...] = total
    ring_step(2)
    arrive(stb)
    S["stc"][z] = jnp.sum(S["stb"][...], axis=0)
    stc = spread("stc", z, "ssc", "z")
    ring_step(3)
    arrive(stc)
    ring_step(4)
    for axis in (0, 1):
        for way in (0, 1):
            ring[axis, way, 3, 1 - way].wait_recv()
            ring[axis, way, 4, way].wait_recv()

    def scale_of(tile):
        mean = tile[0:1] / D
        return mean, lax.rsqrt(tile[1:2] / D - mean * mean + epsilon)

    def normed(tok, carry):
        mean, inv = scale_of(S["stc"][tok])
        for i in range(8):
            S["nt"][tok, i] = ((S["xg"][tok, i].astype(f32) - mean) * inv * S["gb"][i]).astype(bf16)
        return carry

    lax.fori_loop(0, 8, normed, 0)

    def pair(ref, i):
        return jnp.concatenate(
            [ref[2 * i].reshape(K, 128), ref[2 * i + 1].reshape(K, 128)], axis=1)

    for i in range(4):
        lanes = slice(256 * i, 256 * (i + 1))
        pre_part = lax.dot_general(
            S["w1"][...], pair(S["nt"], i), (((0,), (0,)), ((), ())), preferred_element_type=f32)
        act_part = jnp.dot(S["w2"][...], pair(S["tg"], i), preferred_element_type=f32)
        S["part"][0, :, :, :, lanes] = pre_part.reshape(4, 2, Q, 256)
        S["part"][1, :, :, :, lanes] = act_part.reshape(4, 2, Q, 256)

    pairs = []
    for i in (1, 2, 3, 0):
        to = (chip + i) % 4
        for arr in range(2):
            S["cs"][to, arr] = S["part"][arr, to, 1 - core].astype(bf16)
        pairs.append(go(S["cs"].at[to], S["cr"].at[to], "core", (i,), at(2 * chip + 1 - core, z, y)))
    hops = []
    for i in (1, 2, 3):
        to = (chip + i) % 4
        pairs[i - 1].wait_recv()
        for arr in range(2):
            S["xs"][i - 1, arr] = (S["part"][arr, to, core] + S["cr"][to, arr].astype(f32)).astype(bf16)
        hops.append(go(S["xs"].at[i - 1], S["xr"].at[i - 1], "xx", (i - 1,), at(2 * to + core, z, y)))
    pairs[3].wait_recv()
    for arr in range(2):
        S["pre"][arr] = S["part"][arr, chip, core] + S["cr"][chip, arr].astype(f32)
    for i in range(3):
        hops[i].wait_recv()
    pre_act = S["pre"][0] + sum(S["xr"][i, 0].astype(f32) for i in range(3))
    act_grad = S["pre"][1] + sum(S["xr"][i, 1].astype(f32) for i in range(3))
    value, slope = gelu_parts(pre_act)
    pre_grad = (act_grad * slope).astype(bf16)
    S["comb"][d, 0] = value.astype(bf16)
    S["comb"][d, 1] = pre_grad
    second = jnp.sum(pre_grad.astype(f32) * pre_act, axis=0, keepdims=True)

    hops = [
        go(S["comb"].at[d], S["comb"].at[d], "ax", (i - 1,), at(2 * ((chip + i) % 4) + core, z, y))
        for i in (1, 2, 3)]
    pairs = []
    for i in (0, 3, 2, 1):
        slot = 2 * ((chip + i) % 4) + core
        if i:
            hops[3 - i].wait_recv()
        pairs.append(go(
            S["comb"].at[slot], S["comb"].at[slot], "ac", (i,), at(2 * chip + 1 - core, z, y)))
    arrive(pairs)

    for i in range(4):
        lanes = slice(256 * i, 256 * (i + 1))
        out = jnp.dot(S["w1"][...], S["comb"][:, 1, :, lanes].reshape(H, 256), preferred_element_type=f32)
        S["ng"][2 * i] = out[:, :128].reshape(8, F, 128)
        S["ng"][2 * i + 1] = out[:, 128:].reshape(8, F, 128)

    rs = {}

    def rs_block(axis, dest, sub):
        half = pl.ds(4 * sub, 4)
        if axis == 0:
            return S["ng"][half, dest, 0:HALF]
        return S["ng"][dest, half, HALF:F]

    def rs_add(axis, way, k, sub, val):
        if (axis, way, k, sub) in rs:
            rs[axis, way, k, sub].wait_recv()
            val = val + S["ra"][axis, way, k - 1, pl.ds(4 * sub, 4)].astype(f32)
        return val

    def rs_step(k):
        for sub in (0, 1):
            for axis in (0, 1):
                for way in (0, 1):
                    if k == 1 and sub != way:
                        continue
                    sign = 1 - 2 * way
                    me = y if axis == 0 else z
                    val = rs_block(axis, (me + sign * (5 - k) + 8) % 8, sub)
                    val = rs_add(axis, way, k - 1, sub, val)
                    half = pl.ds(4 * sub, 4)
                    S["sa"][axis, way, k - 1, half] = val.astype(bf16)
                    rs[axis, way, k, sub] = go(
                        S["sa"].at[axis, way, k - 1, half], S["ra"].at[axis, way, k - 1, half],
                        "rs", (axis, way, k - 1, sub), along("yz"[axis], sign + 8))

    rs_step(1)
    pg = S["comb"][:, 1].reshape(H, 1024)
    high = S["u"][...].astype(bf16)
    low = (S["u"][...] - high.astype(f32)).astype(bf16)
    first = jnp.dot(high, pg, preferred_element_type=f32) + jnp.dot(low, pg, preferred_element_type=f32)
    S["s2p"][...] = jnp.zeros_like(S["s2p"])
    for i in range(8):
        lanes = slice(128 * i, 128 * (i + 1))
        S["s2p"][i, 0:1] = first[0:1, lanes]
        S["s2p"][i, 1:2] = second[:, lanes]
    s2a = [
        go(S["s2p"].at[(d + i) % 8], S["s2r"].at[d], "s2a", (i - 1,), along("dp", i)) for i in range(1, 8)]
    S["s2r"][d] = S["s2p"][d]
    rs_step(2)
    nt_all = jnp.concatenate([S["nt"][i].reshape(K, 128) for i in range(8)], axis=1)
    S["w1g"][...] = lax.dot_general(nt_all, pg, (((1,), (1,)), ((), ())), preferred_element_type=f32)
    store1 = pltpu.make_async_copy(S["w1g"], w1g_hbm, S["loc"].at[2])
    store1.start()
    arrive(s2a)
    S["s2y"][y] = jnp.sum(S["s2r"][...], axis=0)
    s2b = spread("s2y", y, "s2b", "y")
    rs_step(3)
    tg_all = jnp.concatenate([S["tg"][i].reshape(K, 128) for i in range(8)], axis=1)
    S["w2g"][...] = lax.dot_general(
        S["comb"][:, 0].reshape(H, 1024), tg_all, (((1,), (1,)), ((), ())), preferred_element_type=f32)
    store2 = pltpu.make_async_copy(S["w2g"], w2g_hbm, S["loc"].at[3])
    store2.start()
    arrive(s2b)
    S["s2z"][z] = jnp.sum(S["s2y"][...], axis=0)
    s2c = spread("s2z", z, "s2c", "z")
    rs_step(4)
    arrive(s2c)
    for axis in (0, 1):
        for sub in (0, 1):
            half = pl.ds(4 * sub, 4)
            val = rs_block(axis, y if axis == 0 else z, sub)
            for way in (0, 1):
                val = rs_add(axis, way, 4, sub, val)
            S["fs"][axis, half] = val.astype(bf16)

    fins = []
    for axis in (0, 1):
        for i in range(8):
            if axis == 0:
                step = (d + i) % 8
                dev, slot = at(step, d, y), z
                clear = jnp.logical_or(off_diag, step != d)
            else:
                step = (y + i) % 8
                dev, slot = at(z, d, step), y
                clear = jnp.logical_or(off_diag, step != y)
            copy = remote(S["fs"].at[axis, step], S["fr"].at[axis, slot], "fin", (axis, i), dev, (axis, slot))
            if i:
                copy.start()
            else:
                @pl.when(clear)
                def _():
                    copy.start()

                @pl.when(jnp.logical_not(clear))
                def _():
                    pltpu.make_async_copy(
                        S["fs"].at[axis, step], S["fr"].at[axis, slot], S["fin"].at[1, axis, slot]).start()
            fins.append((copy, i, clear))
    gcol = turned(S["gown"][0:1])[:F]
    mean, inv = scale_of(S["stc"][d])
    cen = (S["own"][0].astype(f32) - mean) * inv
    tile = jnp.sum(S["s2z"][...], axis=0)
    base = S["own"][1].astype(f32) - inv * (tile[0:1] / D + cen * (tile[1:2] / D))
    for axis in (0, 1):
        for slot in range(8):
            remote(S["fs"].at[axis, slot], S["fr"].at[axis, slot], "fin", (axis, slot), at(z, d, y)).wait_recv()
        S["pad"][0, HALF * axis:HALF * (axis + 1)] = jnp.sum(S["fr"][axis].astype(f32), axis=0)
    grad = S["pad"][0, :F]
    S["pad"][1, :F] = grad * cen
    S["ge"][d] = jnp.broadcast_to(jnp.sum(S["pad"][1].T, axis=0, keepdims=True), (8, 128))
    ge = spread("ge", d, "gx", "dp")
    S["pad"][0, :F] = base + inv * (grad * gcol)
    ig_ref[...] = S["pad"][0].T[:, :F].astype(bf16)
    arrive(ge)
    gg_out[...] = jnp.sum(S["ge"][...], axis=0)

    for copy in sends:
        copy.wait_send()
    for copy, i, clear in fins:
        if i:
            copy.wait_send()
        else:
            @pl.when(clear)
            def _():
                copy.wait_send()

    @pl.when(off_diag)
    def _():
        for copy in perm:
            copy.wait_send()

    store1.wait()
    store2.wait()


def shards(inputs, gain, w_in, w_out, targets):
    vmem, hbm = pl.BlockSpec(memory_space=pltpu.VMEM), pl.BlockSpec(memory_space=pl.ANY)
    scratch = [pltpu.VMEM(shape, kind) for shape, kind in SCRATCH.values()]
    scratch += [pltpu.SemaphoreType.DMA(shape) for shape in SEMS.values()]
    input_grad, gain_grad, w_in_grad, w_out_grad = pl.pallas_call(
        kernel,
        out_shape=(
            jax.ShapeDtypeStruct((128, F), bf16), jax.ShapeDtypeStruct((8, 128), f32),
            jax.ShapeDtypeStruct((K, H), f32), jax.ShapeDtypeStruct((H, K), f32)),
        in_specs=[vmem, vmem, vmem, hbm, hbm],
        out_specs=(vmem, vmem, hbm, hbm),
        scratch_shapes=scratch,
        compiler_params=pltpu.CompilerParams(
            collective_id=0, has_side_effects=True, vmem_limit_bytes=48 * 1024 * 1024),
        cost_estimate=pl.CostEstimate(flops=2 * 10 ** 9, bytes_accessed=4 * 10 ** 6, transcendentals=10 ** 5),
        name="backward",
    )(inputs, targets, gain.reshape(1, F), w_in, w_out)
    return input_grad, gain_grad[0, :F], w_in_grad, w_out_grad


def solution(mesh):
    return jax.shard_map(
        shards,
        mesh=mesh,
        in_specs=(P("dp", "mp"), P("mp"), P("dp", "mp"), P("mp", "dp"), P("dp", "mp")),
        out_specs=(P("dp", "mp"), P("mp"), P("dp", "mp"), P("mp", "dp")),
        check_vma=False,
    )
```

```python
import functools

import jax
import jax.numpy as jnp
from jax import lax
from jax.experimental import pallas as pl
from jax.experimental.pallas import tpu as pltpu
from jax.sharding import PartitionSpec as P

epsilon = 1e-06
MESH = pl.DeviceIdType.MESH
bf16, f32 = jnp.bfloat16, jnp.float32
D = 6144
F = 96
K = 768
H = 256
Q = 32
HALF = F // 2


def gelu_parts(values):
    cumul = 0.5 * (1.0 + lax.erf(values * 0.7071067811865476))
    slope = cumul + values * jnp.exp(-0.5 * values * values) * 0.3989422804014327
    return values * cumul, slope


def when_wait(cond, copy):
    @pl.when(cond)
    def _():
        copy.wait_send()


def turned(rows):
    return jnp.broadcast_to(rows, (128, 128)).T


SCRATCH = dict(
    w1=((K, H), bf16), w2=((H, K), bf16),
    pad=((128, 128), f32), gown=((8, 128), f32),
    xg=((8, 8, F, 128), bf16), tg=((8, 8, F, 128), bf16), nt=((8, 8, F, 128), bf16),
    gg=((8, 8, 128), f32), gb=((8, F, 128), f32),
    sta=((8, 8, 128), f32), stb=((8, 8, 128), f32), stc=((8, 8, 128), f32),
    part=((2, 4, 2, Q, 1024), f32), cs=((4, 2, Q, 1024), bf16), cr=((4, 2, Q, 1024), bf16),
    xs=((3, 2, Q, 1024), bf16), xr=((3, 2, Q, 1024), bf16),
    pre=((2, Q, 1024), f32), comb=((8, 2, Q, 1024), bf16),
    u=((8, H), f32), s2p=((8, 8, 128), f32), s2r=((8, 8, 128), f32),
    s2y=((8, 8, 128), f32), s2z=((8, 8, 128), f32),
    ng=((8, 8, F, 128), f32), ra=((2, 2, 4, 8, HALF, 128), bf16), sa=((2, 2, 4, 8, HALF, 128), bf16),
    fs=((2, 8, HALF, 128), bf16), fr=((2, 8, HALF, 128), bf16),
    w1g=((K, H), f32), w2g=((H, K), f32), ge=((8, 8, 128), f32),
)
SEMS = dict(
    loc=(4,), perm=(2, 3), sx=(2, 7), stg=(2, 7), small=(2, 10), ring_s=(2, 4), ring_r=(2, 2, 4, 4),
    core=(2, 4), xx=(2, 3), ax=(2, 3), ac=(2, 4), rs=(2, 2, 2, 4, 2), fin_s=(2, 2), fin_r=(2,),
)


LAST = None


def kernel(*refs):
    ends = []
    for name in phases(ends, *refs):
        if name == LAST:
            break
    for end in ends:
        end()


def phases(ends, x_ref, t_ref, g_ref, w1_hbm, w2_hbm, ig_ref, gg_out, w1g_hbm, w2g_hbm, *scratch):
    S = dict(zip(list(SCRATCH) + list(SEMS), scratch, strict=True))
    d, m = lax.axis_index("dp"), lax.axis_index("mp")
    z, y = m // 8, m % 8
    chip, core = d // 2, d % 2
    diag = d == z
    off_diag = jnp.logical_not(diag)

    def at(dp, zz, yy):
        return (dp, zz * 8 + yy)

    def remote(src, dst, sem, index, dev):
        return pltpu.make_async_remote_copy(
            src_ref=src, dst_ref=dst, send_sem=S[sem].at[(0, *index)],
            recv_sem=S[sem].at[(1, *index)], device_id=dev, device_id_type=MESH)

    def whole(ref, send_sem, recv_sem):
        return pltpu.make_async_remote_copy(
            src_ref=ref, dst_ref=ref, send_sem=send_sem, recv_sem=recv_sem,
            device_id=at(z, d, y), device_id_type=MESH)

    def go(src, dst, sem, index, dev):
        copy = remote(src, dst, sem, index, dev)
        copy.start()
        ends.append(copy.wait_send)
        return copy

    def along(axis, i):
        if axis == "dp":
            return at((d + i) % 8, z, y)
        if axis == "z":
            return at(d, (z + i) % 8, y)
        return at(d, z, (y + i) % 8)

    def spread(buf, slot, number, axis, source=None):
        for i in range(1, 8):
            src = S[buf].at[slot] if source is None else source(i)
            remote(src, S[buf].at[slot], "small", (number,), along(axis, i)).start()
        seven = whole(S[buf].at[pl.ds(0, 7)], S["small"].at[0, number], S["small"].at[1, number])
        ends.append(seven.wait_send)
        return [seven]

    def arrive(copies):
        for copy in copies:
            copy.wait_recv()

    load1 = pltpu.make_async_copy(w1_hbm, S["w1"], S["loc"].at[0])
    load2 = pltpu.make_async_copy(w2_hbm, S["w2"], S["loc"].at[1])
    load1.start()
    load2.start()
    loads = [load1.wait, load2.wait]
    ends.extend(loads)

    barrier = pltpu.get_barrier_semaphore()

    def hail(dev):
        pl.semaphore_signal(barrier, inc=1, device_id=dev, device_id_type=MESH)

    for axis in ("dp", "z", "y"):
        for i in range(1, 8):
            hail(along(axis, i))

    @pl.when(off_diag)
    def _():
        hail(at(z, d, y))

    S["pad"][...] = jnp.zeros_like(S["pad"])
    S["gown"][...] = jnp.zeros_like(S["gown"])
    S["gown"][:, :F] = jnp.broadcast_to(g_ref[...].astype(f32), (8, F))

    @pl.when(off_diag)
    def _():
        pl.semaphore_wait(barrier, 22)

    @pl.when(diag)
    def _():
        pl.semaphore_wait(barrier, 21)

    if LAST == "barrier":
        return

    perm = [
        (x_ref, S["xg"].at[d, y]),
        (t_ref, S["tg"].at[d, y]),
        (S["gown"], S["gg"].at[y]),
    ]
    perm = [remote(src, dst, "perm", (i,), at(z, d, y)) for i, (src, dst) in enumerate(perm)]

    @pl.when(off_diag)
    def _():
        for copy in perm:
            copy.start()

    @pl.when(diag)
    def _():
        pltpu.make_async_copy(x_ref, S["xg"].at[z, y], S["perm"].at[1, 0]).start()
        pltpu.make_async_copy(t_ref, S["tg"].at[z, y], S["perm"].at[1, 1]).start()
        pltpu.make_async_copy(S["gown"], S["gg"].at[y], S["perm"].at[1, 2]).start()

    @ends.append
    def _():
        @pl.when(off_diag)
        def _():
            for copy in perm:
                copy.wait_send()

    arrive(perm)
    yield "permute"

    gx = [
        go(S["xg"].at[z, y], S["xg"].at[z, y], "sx", (i - 1,), along("z", i)) for i in range(1, 8)]
    gt = [go(S["tg"].at[z, y], S["tg"].at[z, y], "stg", (i - 1,), along("y", i)) for i in range(1, 8)]
    ggain = spread("gg", y, 0, "y")
    piece = S["xg"][z, y].astype(f32)
    S["sta"][y] = jnp.zeros((8, 128), f32)
    S["sta"][y, 0:1] = jnp.sum(piece, axis=0, keepdims=True)
    S["sta"][y, 1:2] = jnp.sum(piece * piece, axis=0, keepdims=True)
    sta = spread("sta", y, 1, "y")
    def offset(e):
        return (e + 1) // 2 if e % 2 else (8 - e // 2) % 8

    def ring_piece(axis, origin, e):
        if isinstance(e, int):
            off = offset(e)
        else:
            off = jnp.where(e % 2 == 1, (e + 1) // 2, (8 - e // 2) % 8)
        if axis == 0:
            return S["xg"].at[(z + off) % 8, origin]
        return S["tg"].at[origin, (y + off) % 8]

    def ring_send(axis, way, k, j, p):
        sign = 1 - 2 * way
        ref = ring_piece(axis, ((y if axis == 0 else z) - sign * (k - 1) + 8) % 8, 2 * j + p)
        pltpu.make_async_remote_copy(
            src_ref=ref, dst_ref=ref, send_sem=S["ring_s"].at[axis, k - 1],
            recv_sem=S["ring_r"].at[axis, way, k - 1, j],
            device_id=along("yz"[axis], sign + 8), device_id_type=MESH).start()

    def ring_wait(axis, way, k, j):
        whole(S["xg"].at[0, pl.ds(0, 2)], S["ring_s"].at[axis, 0], S["ring_r"].at[axis, way, k - 1, j]).wait_recv()

    def ring_rest(k, j, carry):
        for axis in (0, 1):
            for way in (0, 1):
                ring_wait(axis, way, k - 1, j)
                for p in (0, 1):
                    ring_send(axis, way, k, j, p)
        return carry

    def ring_last(j, carry):
        for axis in (0, 1):
            for way in (0, 1):
                ring_wait(axis, way, 3, 2 * j + way)
                for p in (0, 1):
                    ring_send(axis, way, 4, 2 * j + way, p)
        return carry

    for e in range(8):
        for axis in (0, 1):
            if e:
                (gx, gt)[axis][7 - offset(e)].wait_recv()
            for way in (0, 1):
                ring_send(axis, way, 1, e // 2, e % 2)
    for axis in (0, 1):
        for k in (1, 2, 3, 4):
            ends.append(whole(
                S["xg"].at[pl.ds(0, 2)] if k < 4 else S["xg"].at[0],
                S["ring_s"].at[axis, k - 1], S["ring_r"].at[axis, 0, 0, 0]).wait_send)
    arrive(sta)
    S["stb"][d] = jnp.sum(S["sta"][...], axis=0)
    stb = spread("stb", d, 2, "dp")
    arrive(ggain)
    for load in loads:
        load()
        ends.remove(load)
    total = jnp.zeros((8, H), f32)
    for i in range(8):
        rows = S["gg"][i]
        S["gb"][i] = turned(rows[0:1])[:F]
        total += jnp.dot(rows[:, :F].astype(bf16), S["w1"][F * i:F * (i + 1)], preferred_element_type=f32)
    S["u"][...] = total
    lax.fori_loop(0, 4, functools.partial(ring_rest, 2), 0)
    arrive(stb)
    S["stc"][z] = jnp.sum(S["stb"][...], axis=0)
    stc = spread("stc", z, 3, "z")
    lax.fori_loop(0, 4, functools.partial(ring_rest, 3), 0)
    arrive(stc)
    lax.fori_loop(0, 2, ring_last, 0)
    for axis in (0, 1):
        for way in (0, 1):
            for j in (0, 1):
                ring_wait(axis, way, 3, 2 * j + 1 - way)
                ring_wait(axis, way, 4, 2 * j + way)
    yield "ring"

    def scale_of(tile):
        mean = tile[0:1] / D
        return mean, lax.rsqrt(tile[1:2] / D - mean * mean + epsilon)

    def normed(tok, carry):
        mean, inv = scale_of(S["stc"][tok])
        for i in range(8):
            S["nt"][tok, i] = ((S["xg"][tok, i].astype(f32) - mean) * inv * S["gb"][i]).astype(bf16)
        return carry

    lax.fori_loop(0, 8, normed, 0)

    def pair(ref, i):
        return jnp.concatenate(
            [ref[2 * i].reshape(K, 128), ref[2 * i + 1].reshape(K, 128)], axis=1)

    for i in range(4):
        lanes = slice(256 * i, 256 * (i + 1))
        pre_part = lax.dot_general(
            S["w1"][...], pair(S["nt"], i), (((0,), (0,)), ((), ())), preferred_element_type=f32)
        act_part = jnp.dot(S["w2"][...], pair(S["tg"], i), preferred_element_type=f32)
        S["part"][0, :, :, :, lanes] = pre_part.reshape(4, 2, Q, 256)
        S["part"][1, :, :, :, lanes] = act_part.reshape(4, 2, Q, 256)

    yield "products"

    pairs = []
    for i in (1, 2, 3, 0):
        to = (chip + i) % 4
        for arr in range(2):
            S["cs"][to, arr] = S["part"][arr, to, 1 - core].astype(bf16)
        pairs.append(go(S["cs"].at[to], S["cr"].at[to], "core", (i,), at(2 * chip + 1 - core, z, y)))
    hops = []
    for i in (1, 2, 3):
        to = (chip + i) % 4
        pairs[i - 1].wait_recv()
        for arr in range(2):
            S["xs"][i - 1, arr] = (S["part"][arr, to, core] + S["cr"][to, arr].astype(f32)).astype(bf16)
        hops.append(go(S["xs"].at[i - 1], S["xr"].at[i - 1], "xx", (i - 1,), at(2 * to + core, z, y)))
    pairs[3].wait_recv()
    for arr in range(2):
        S["pre"][arr] = S["part"][arr, chip, core] + S["cr"][chip, arr].astype(f32)
    for i in range(3):
        hops[i].wait_recv()
    pre_act = S["pre"][0] + sum(S["xr"][i, 0].astype(f32) for i in range(3))
    act_grad = S["pre"][1] + sum(S["xr"][i, 1].astype(f32) for i in range(3))
    value, slope = gelu_parts(pre_act)
    pre_grad = (act_grad * slope).astype(bf16)
    S["comb"][d, 0] = value.astype(bf16)
    S["comb"][d, 1] = pre_grad
    yield "dpsum"
    second = jnp.sum(pre_grad.astype(f32) * pre_act, axis=0, keepdims=True)

    hops = [
        go(S["comb"].at[d], S["comb"].at[d], "ax", (i - 1,), at(2 * ((chip + i) % 4) + core, z, y))
        for i in (1, 2, 3)]
    pairs = []
    for i in (0, 3, 2, 1):
        slot = 2 * ((chip + i) % 4) + core
        if i:
            hops[3 - i].wait_recv()
        pairs.append(go(
            S["comb"].at[slot], S["comb"].at[slot], "ac", (i,), at(2 * chip + 1 - core, z, y)))
    arrive(pairs)

    yield "dpgather"

    for i in range(4):
        lanes = slice(256 * i, 256 * (i + 1))
        out = jnp.dot(S["w1"][...], S["comb"][:, 1, :, lanes].reshape(H, 256), preferred_element_type=f32)
        S["ng"][2 * i] = out[:, :128].reshape(8, F, 128)
        S["ng"][2 * i + 1] = out[:, 128:].reshape(8, F, 128)

    rs = {}

    def rs_block(axis, dest, sub):
        half = pl.ds(4 * sub, 4)
        if axis == 0:
            return S["ng"][half, dest, 0:HALF]
        return S["ng"][dest, half, HALF:F]

    def rs_add(axis, way, k, sub, val):
        if (axis, way, k, sub) in rs:
            rs[axis, way, k, sub].wait_recv()
            val = val + S["ra"][axis, way, k - 1, pl.ds(4 * sub, 4)].astype(f32)
        return val

    def rs_step(k):
        for sub in (0, 1):
            for axis in (0, 1):
                for way in (0, 1):
                    if k == 1 and sub != way:
                        continue
                    sign = 1 - 2 * way
                    me = y if axis == 0 else z
                    val = rs_block(axis, (me + sign * (5 - k) + 8) % 8, sub)
                    val = rs_add(axis, way, k - 1, sub, val)
                    half = pl.ds(4 * sub, 4)
                    S["sa"][axis, way, k - 1, half] = val.astype(bf16)
                    rs[axis, way, k, sub] = go(
                        S["sa"].at[axis, way, k - 1, half], S["ra"].at[axis, way, k - 1, half],
                        "rs", (axis, way, k - 1, sub), along("yz"[axis], sign + 8))

    rs_step(1)
    pg = S["comb"][:, 1].reshape(H, 1024)
    high = S["u"][...].astype(bf16)
    low = (S["u"][...] - high.astype(f32)).astype(bf16)
    first = jnp.dot(high, pg, preferred_element_type=f32) + jnp.dot(low, pg, preferred_element_type=f32)
    S["s2p"][...] = jnp.zeros_like(S["s2p"])
    for i in range(8):
        lanes = slice(128 * i, 128 * (i + 1))
        S["s2p"][i, 0:1] = first[0:1, lanes]
        S["s2p"][i, 1:2] = second[:, lanes]
    s2a = spread("s2r", d, 4, "dp", lambda i: S["s2p"].at[(d + i) % 8])
    S["s2r"][d] = S["s2p"][d]
    rs_step(2)
    nt_all = jnp.concatenate([S["nt"][i].reshape(K, 128) for i in range(8)], axis=1)
    S["w1g"][...] = lax.dot_general(nt_all, pg, (((1,), (1,)), ((), ())), preferred_element_type=f32)
    store1 = pltpu.make_async_copy(S["w1g"], w1g_hbm, S["loc"].at[2])
    store1.start()
    ends.append(store1.wait)
    arrive(s2a)
    S["s2y"][y] = jnp.sum(S["s2r"][...], axis=0)
    s2b = spread("s2y", y, 5, "y")
    rs_step(3)
    tg_all = jnp.concatenate([S["tg"][i].reshape(K, 128) for i in range(8)], axis=1)
    S["w2g"][...] = lax.dot_general(
        S["comb"][:, 0].reshape(H, 1024), tg_all, (((1,), (1,)), ((), ())), preferred_element_type=f32)
    store2 = pltpu.make_async_copy(S["w2g"], w2g_hbm, S["loc"].at[3])
    store2.start()
    ends.append(store2.wait)
    arrive(s2b)
    S["s2z"][z] = jnp.sum(S["s2y"][...], axis=0)
    s2c = spread("s2z", z, 6, "z")
    rs_step(4)
    arrive(s2c)
    for axis in (0, 1):
        for sub in (0, 1):
            half = pl.ds(4 * sub, 4)
            val = rs_block(axis, y if axis == 0 else z, sub)
            for way in (0, 1):
                val = rs_add(axis, way, 4, sub, val)
            S["fs"][axis, half] = val.astype(bf16)

    yield "rings"

    for axis in (0, 1):
        for i in range(8):
            if axis == 0:
                step = (d + i) % 8
                dev, slot = at(step, d, y), z
                clear = jnp.logical_or(off_diag, step != d)
            else:
                step = (y + i) % 8
                dev, slot = at(z, d, step), y
                clear = jnp.logical_or(off_diag, step != y)
            copy = pltpu.make_async_remote_copy(
                src_ref=S["fs"].at[axis, step], dst_ref=S["fr"].at[axis, slot],
                send_sem=S["fin_s"].at[axis, int(i > 0)], recv_sem=S["fin_r"].at[axis],
                device_id=dev, device_id_type=MESH)
            if i:
                copy.start()
            else:
                @pl.when(clear)
                def _():
                    copy.start()

                @pl.when(jnp.logical_not(clear))
                def _():
                    pltpu.make_async_copy(
                        S["fs"].at[axis, step], S["fr"].at[axis, slot], S["fin_r"].at[axis]).start()
                ends.append(functools.partial(when_wait, clear, copy))
        ends.append(whole(S["fs"].at[axis, pl.ds(0, 7)], S["fin_s"].at[axis, 1], S["fin_r"].at[axis]).wait_send)
    gcol = turned(S["gown"][0:1])[:F]
    mean, inv = scale_of(S["stc"][d])
    cen = (x_ref[...].astype(f32) - mean) * inv
    tile = jnp.sum(S["s2z"][...], axis=0)
    base = t_ref[...].astype(f32) - inv * (tile[0:1] / D + cen * (tile[1:2] / D))
    for axis in (0, 1):
        whole(S["fr"].at[axis], S["fin_s"].at[axis, 1], S["fin_r"].at[axis]).wait_recv()
    grad = jnp.concatenate([jnp.sum(S["fr"][axis].astype(f32), axis=0) for axis in (0, 1)], axis=0)
    S["pad"][:F] = grad * cen
    S["ge"][d] = jnp.broadcast_to(jnp.sum(S["pad"][...].T, axis=0, keepdims=True), (8, 128))
    ge = spread("ge", d, 7, "dp")
    ig_ref[...] = (base + inv * (grad * gcol)).astype(bf16)
    arrive(ge)
    gg_out[...] = jnp.sum(S["ge"][...], axis=0)


def shards(inputs, gain, w_in, w_out, targets):
    vmem, hbm = pl.BlockSpec(memory_space=pltpu.VMEM), pl.BlockSpec(memory_space=pl.ANY)
    scratch = [pltpu.VMEM(shape, kind) for shape, kind in SCRATCH.values()]
    scratch += [pltpu.SemaphoreType.DMA(shape) for shape in SEMS.values()]
    input_grad, gain_grad, w_in_grad, w_out_grad = pl.pallas_call(
        kernel,
        out_shape=(
            jax.ShapeDtypeStruct((F, 128), bf16), jax.ShapeDtypeStruct((8, 128), f32),
            jax.ShapeDtypeStruct((K, H), f32), jax.ShapeDtypeStruct((H, K), f32)),
        in_specs=[vmem, vmem, vmem, hbm, hbm],
        out_specs=(vmem, vmem, hbm, hbm),
        scratch_shapes=scratch,
        compiler_params=pltpu.CompilerParams(
            collective_id=0, has_side_effects=True, vmem_limit_bytes=60 * 1024 * 1024),
        cost_estimate=pl.CostEstimate(flops=2 * 10 ** 9, bytes_accessed=4 * 10 ** 6, transcendentals=10 ** 5),
        name="backward",
    )(inputs.T, targets.T, gain.reshape(1, F), w_in, w_out)
    return input_grad.T, gain_grad[0, :F], w_in_grad, w_out_grad


def solution(mesh):
    return jax.shard_map(
        shards,
        mesh=mesh,
        in_specs=(P("dp", "mp"), P("mp"), P("dp", "mp"), P("mp", "dp"), P("dp", "mp")),
        out_specs=(P("dp", "mp"), P("mp"), P("dp", "mp"), P("mp", "dp")),
        check_vma=False,
    )
```

```python
import functools

import jax
import jax.numpy as jnp
from jax import lax
from jax.experimental import pallas as pl
from jax.experimental.pallas import tpu as pltpu
from jax.sharding import PartitionSpec as P

epsilon = 1e-06
MESH = pl.DeviceIdType.MESH
bf16, f32 = jnp.bfloat16, jnp.float32
D = 6144
F = 96
K = 768
H = 256
Q = 32
HALF = F // 2


def gelu_parts(values):
    cumul = 0.5 * (1.0 + lax.erf(values * 0.7071067811865476))
    slope = cumul + values * jnp.exp(-0.5 * values * values) * 0.3989422804014327
    return values * cumul, slope


def when_wait(cond, copy):
    @pl.when(cond)
    def _():
        copy.wait_send()


def turned(rows):
    return jnp.broadcast_to(rows, (128, 128)).T


SCRATCH = dict(
    w1=((K, H), bf16), w2=((H, K), bf16),
    pad=((128, 128), f32), gown=((8, 128), f32),
    xg=((8, 8, F, 128), bf16), tg=((8, 8, F, 128), bf16), nt=((8, 8, F, 128), bf16),
    gg=((8, 8, 128), f32), gb=((8, F, 128), f32),
    sta=((8, 8, 128), f32), stb=((8, 8, 128), f32), stc=((8, 8, 128), f32),
    part=((2, 2, 4, 2, Q, 512), f32), cs=((2, 4, 2, Q, 512), bf16), cr=((2, 4, 2, Q, 512), bf16),
    xs=((2, 3, 2, Q, 512), bf16), xr=((2, 3, 2, Q, 512), bf16), comb=((2, 8, 2, Q, 512), bf16),
    u=((8, H), f32), s2p=((8, 8, 128), f32), s2r=((8, 8, 128), f32),
    s2y=((8, 8, 128), f32), s2z=((8, 8, 128), f32),
    ng=((8, 8, F, 128), f32), ra=((2, 2, 4, 8, HALF, 128), bf16), sa=((2, 2, 4, 8, HALF, 128), bf16),
    fs=((8, 2, HALF, 128), bf16), ft=((8, 2, HALF, 128), bf16), fr=((2, 8, HALF, 128), bf16),
    w1g=((K, H), f32), w2g=((H, K), f32), gs=((8, 8, 128), f32), gr=((2, 8, 8, 128), f32),
)
SEMS = dict(
    loc=(4,), perm=(2, 3), sx=(2, 7), stg=(2, 7), small=(2, 10), ring_s=(2, 4), ring_r=(2, 2, 4, 4),
    core=(2, 2, 4), xx=(2, 2, 3), ax=(2, 2, 3), ac=(2, 2, 4), rs=(2, 2, 2, 4, 2), fin=(2, 6),
)


LAST = None


def kernel(*refs):
    ends = []
    for name in phases(ends, *refs):
        if name == LAST:
            break
    for end in ends:
        end()


def phases(ends, x_ref, t_ref, g_ref, w1_hbm, w2_hbm, ig_ref, gg_out, w1g_hbm, w2g_hbm, *scratch):
    S = dict(zip(list(SCRATCH) + list(SEMS), scratch, strict=True))
    d, m = lax.axis_index("dp"), lax.axis_index("mp")
    z, y = m // 8, m % 8
    chip, core = d // 2, d % 2
    diag = d == z
    off_diag = jnp.logical_not(diag)

    def at(dp, zz, yy):
        return (dp, zz * 8 + yy)

    def remote(src, dst, sem, index, dev):
        return pltpu.make_async_remote_copy(
            src_ref=src, dst_ref=dst, send_sem=S[sem].at[(0, *index)],
            recv_sem=S[sem].at[(1, *index)], device_id=dev, device_id_type=MESH)

    def whole(ref, send_sem, recv_sem):
        return pltpu.make_async_remote_copy(
            src_ref=ref, dst_ref=ref, send_sem=send_sem, recv_sem=recv_sem,
            device_id=at(z, d, y), device_id_type=MESH)

    def go(src, dst, sem, index, dev):
        copy = remote(src, dst, sem, index, dev)
        copy.start()
        ends.append(copy.wait_send)
        return copy

    def along(axis, i):
        if axis == "dp":
            return at((d + i) % 8, z, y)
        if axis == "z":
            return at(d, (z + i) % 8, y)
        return at(d, z, (y + i) % 8)

    def spread(buf, slot, number, axis, source=None):
        for i in range(1, 8):
            src = S[buf].at[slot] if source is None else source(i)
            remote(src, S[buf].at[slot], "small", (number,), along(axis, i)).start()
        seven = whole(S[buf].at[pl.ds(0, 7)], S["small"].at[0, number], S["small"].at[1, number])
        ends.append(seven.wait_send)
        return [seven]

    def arrive(copies):
        for copy in copies:
            copy.wait_recv()

    load1 = pltpu.make_async_copy(w1_hbm, S["w1"], S["loc"].at[0])
    load2 = pltpu.make_async_copy(w2_hbm, S["w2"], S["loc"].at[1])
    load1.start()
    load2.start()
    loads = [load1.wait, load2.wait]
    ends.extend(loads)

    barrier = pltpu.get_barrier_semaphore()

    def hail(dev):
        pl.semaphore_signal(barrier, inc=1, device_id=dev, device_id_type=MESH)

    for axis in ("dp", "z", "y"):
        for i in range(1, 8):
            hail(along(axis, i))

    @pl.when(off_diag)
    def _():
        hail(at(z, d, y))

    S["pad"][...] = jnp.zeros_like(S["pad"])
    S["gown"][...] = jnp.zeros_like(S["gown"])
    S["gown"][:, :F] = jnp.broadcast_to(g_ref[...].astype(f32), (8, F))

    @pl.when(off_diag)
    def _():
        pl.semaphore_wait(barrier, 22)

    @pl.when(diag)
    def _():
        pl.semaphore_wait(barrier, 21)

    if LAST == "barrier":
        return

    perm = [
        (x_ref, S["xg"].at[d, y]),
        (t_ref, S["tg"].at[d, y]),
        (S["gown"], S["gg"].at[y]),
    ]
    perm = [remote(src, dst, "perm", (i,), at(z, d, y)) for i, (src, dst) in enumerate(perm)]

    @pl.when(off_diag)
    def _():
        for copy in perm:
            copy.start()

    @pl.when(diag)
    def _():
        pltpu.make_async_copy(x_ref, S["xg"].at[z, y], S["perm"].at[1, 0]).start()
        pltpu.make_async_copy(t_ref, S["tg"].at[z, y], S["perm"].at[1, 1]).start()
        pltpu.make_async_copy(S["gown"], S["gg"].at[y], S["perm"].at[1, 2]).start()

    @ends.append
    def _():
        @pl.when(off_diag)
        def _():
            for copy in perm:
                copy.wait_send()

    arrive(perm)
    yield "permute"

    gx = [
        go(S["xg"].at[z, y], S["xg"].at[z, y], "sx", (i - 1,), along("z", i)) for i in range(1, 8)]
    gt = [go(S["tg"].at[z, y], S["tg"].at[z, y], "stg", (i - 1,), along("y", i)) for i in range(1, 8)]
    ggain = spread("gg", y, 0, "y")
    piece = S["xg"][z, y].astype(f32)
    S["sta"][y] = jnp.zeros((8, 128), f32)
    S["sta"][y, 0:1] = jnp.sum(piece, axis=0, keepdims=True)
    S["sta"][y, 1:2] = jnp.sum(piece * piece, axis=0, keepdims=True)
    sta = spread("sta", y, 1, "y")
    def offset(e):
        return (e + 1) // 2 if e % 2 else (8 - e // 2) % 8

    def ring_piece(axis, origin, e):
        if isinstance(e, int):
            off = offset(e)
        else:
            off = jnp.where(e % 2 == 1, (e + 1) // 2, (8 - e // 2) % 8)
        if axis == 0:
            return S["xg"].at[(z + off) % 8, origin]
        return S["tg"].at[origin, (y + off) % 8]

    def ring_send(axis, way, k, j, p):
        sign = 1 - 2 * way
        ref = ring_piece(axis, ((y if axis == 0 else z) - sign * (k - 1) + 8) % 8, 2 * j + p)
        pltpu.make_async_remote_copy(
            src_ref=ref, dst_ref=ref, send_sem=S["ring_s"].at[axis, k - 1],
            recv_sem=S["ring_r"].at[axis, way, k - 1, j],
            device_id=along("yz"[axis], sign + 8), device_id_type=MESH).start()

    def ring_wait(axis, way, k, j):
        whole(S["xg"].at[0, pl.ds(0, 2)], S["ring_s"].at[axis, 0], S["ring_r"].at[axis, way, k - 1, j]).wait_recv()

    def ring_rest(k, j, carry):
        for axis in (0, 1):
            for way in (0, 1):
                ring_wait(axis, way, k - 1, j)
                for p in (0, 1):
                    ring_send(axis, way, k, j, p)
        return carry

    def ring_last(j, carry):
        for axis in (0, 1):
            for way in (0, 1):
                ring_wait(axis, way, 3, 2 * j + way)
                for p in (0, 1):
                    ring_send(axis, way, 4, 2 * j + way, p)
        return carry

    for e in range(8):
        for axis in (0, 1):
            if e:
                (gx, gt)[axis][7 - offset(e)].wait_recv()
            for way in (0, 1):
                ring_send(axis, way, 1, e // 2, e % 2)
    for axis in (0, 1):
        for k in (1, 2, 3, 4):
            ends.append(whole(
                S["xg"].at[pl.ds(0, 2)] if k < 4 else S["xg"].at[0],
                S["ring_s"].at[axis, k - 1], S["ring_r"].at[axis, 0, 0, 0]).wait_send)
    arrive(sta)
    S["stb"][d] = jnp.sum(S["sta"][...], axis=0)
    stb = spread("stb", d, 2, "dp")
    arrive(ggain)
    for load in loads:
        load()
        ends.remove(load)
    total = jnp.zeros((8, H), f32)
    for i in range(8):
        rows = S["gg"][i]
        S["gb"][i] = turned(rows[0:1])[:F]
        total += jnp.dot(rows[:, :F].astype(bf16), S["w1"][F * i:F * (i + 1)], preferred_element_type=f32)
    S["u"][...] = total
    lax.fori_loop(0, 4, functools.partial(ring_rest, 2), 0)
    arrive(stb)
    S["stc"][z] = jnp.sum(S["stb"][...], axis=0)
    stc = spread("stc", z, 3, "z")
    lax.fori_loop(0, 4, functools.partial(ring_rest, 3), 0)
    arrive(stc)
    lax.fori_loop(0, 2, ring_last, 0)
    for axis in (0, 1):
        for way in (0, 1):
            for j in (0, 1):
                ring_wait(axis, way, 3, 2 * j + 1 - way)
                ring_wait(axis, way, 4, 2 * j + way)
    yield "ring"

    def scale_of(tile):
        mean = tile[0:1] / D
        return mean, lax.rsqrt(tile[1:2] / D - mean * mean + epsilon)

    def normed(tok, carry):
        mean, inv = scale_of(S["stc"][tok])
        for i in range(8):
            S["nt"][tok, i] = ((S["xg"][tok, i].astype(f32) - mean) * inv * S["gb"][i]).astype(bf16)
        return carry

    lax.fori_loop(0, 8, normed, 0)

    def pair(ref, i):
        return jnp.concatenate(
            [ref[2 * i].reshape(K, 128), ref[2 * i + 1].reshape(K, 128)], axis=1)

    def products(h):
        for i in (2 * h, 2 * h + 1):
            lanes = slice(256 * (i % 2), 256 * (i % 2 + 1))
            pre_part = lax.dot_general(
                S["w1"][...], pair(S["nt"], i), (((0,), (0,)), ((), ())), preferred_element_type=f32)
            act_part = jnp.dot(S["w2"][...], pair(S["tg"], i), preferred_element_type=f32)
            S["part"][h, 0, :, :, :, lanes] = pre_part.reshape(4, 2, Q, 256)
            S["part"][h, 1, :, :, :, lanes] = act_part.reshape(4, 2, Q, 256)
        pairs = {}
        for i in (1, 2, 3, 0):
            to = (chip + i) % 4
            for arr in range(2):
                S["cs"][h, to, arr] = S["part"][h, arr, to, 1 - core].astype(bf16)
            pairs[i] = go(S["cs"].at[h, to], S["cr"].at[h, to], "core", (h, i), at(2 * chip + 1 - core, z, y))
        return pairs

    def chip_sum(h, pairs):
        hops = []
        for i in (1, 2, 3):
            to = (chip + i) % 4
            pairs[i].wait_recv()
            for arr in range(2):
                S["xs"][h, i - 1, arr] = (
                    S["part"][h, arr, to, core] + S["cr"][h, to, arr].astype(f32)).astype(bf16)
            hops.append(go(S["xs"].at[h, i - 1], S["xr"].at[h, i - 1], "xx", (h, i - 1), at(2 * to + core, z, y)))
        return hops

    def activate(h, pairs, hops):
        pairs[0].wait_recv()
        arrive(hops)
        pre_act, act_grad = (
            S["part"][h, arr, chip, core] + S["cr"][h, chip, arr].astype(f32)
            + sum(S["xr"][h, i, arr].astype(f32) for i in range(3)) for arr in range(2))
        value, slope = gelu_parts(pre_act)
        pre_grad = (act_grad * slope).astype(bf16)
        S["comb"][h, d, 0] = value.astype(bf16)
        S["comb"][h, d, 1] = pre_grad
        hops = {
            i: go(S["comb"].at[h, d], S["comb"].at[h, d], "ax", (h, i - 1), at(2 * ((chip + i) % 4) + core, z, y))
            for i in (1, 2, 3)}
        second = jnp.sum(pre_grad.astype(f32) * pre_act, axis=0, keepdims=True)
        for i in range(4):
            S["s2p"][4 * h + i] = jnp.zeros((8, 128), f32)
            S["s2p"][4 * h + i, 1:2] = second[:, 128 * i:128 * (i + 1)]
        return hops

    def pass_on(h, hops):
        pairs = []
        for i in (0, 3, 1, 2):
            slot = 2 * ((chip - i + 4) % 4) + core
            if i:
                hops[i].wait_recv()
            ref = S["comb"].at[h, slot]
            pairs.append(go(ref, ref, "ac", (h, i), at(2 * chip + 1 - core, z, y)))
        return pairs

    both = (0, 1)
    pairs = [products(h) for h in both]
    yield "products"
    hops = [chip_sum(h, pairs[h]) for h in both]
    hops = [activate(h, pairs[h], hops[h]) for h in both]
    yield "dpsum"
    pairs = [pass_on(h, hops[h]) for h in both]

    def norm_products(h):
        arrive(pairs[h])
        for i in (2 * h, 2 * h + 1):
            lanes = slice(256 * (i % 2), 256 * (i % 2 + 1))
            out = jnp.dot(
                S["w1"][...], S["comb"][h, :, 1, :, lanes].reshape(H, 256), preferred_element_type=f32)
            S["ng"][2 * i] = out[:, :128].reshape(8, F, 128)
            S["ng"][2 * i + 1] = out[:, 128:].reshape(8, F, 128)

    rs = {}

    def rs_block(axis, dest, h):
        return S["ng"][pl.ds(4 * h, 4), dest, HALF * axis:HALF * (axis + 1)]

    def rs_add(axis, way, k, h, val):
        if (axis, way, k, h) in rs:
            rs[axis, way, k, h].wait_recv()
            val = val + S["ra"][axis, way, k - 1, pl.ds(4 * h, 4)].astype(f32)
        return val

    def rs_round(r, h):
        for axis in both:
            for way in both:
                k = r + 1 if h == way else r + 2
                if k > 4:
                    continue
                sign = 1 - 2 * way
                me = y if axis == 0 else z
                val = rs_block(axis, (me + sign * (5 - k) + 8) % 8, h)
                val = rs_add(axis, way, k - 1, h, val)
                half = pl.ds(4 * h, 4)
                S["sa"][axis, way, k - 1, half] = val.astype(bf16)
                rs[axis, way, k, h] = go(
                    S["sa"].at[axis, way, k - 1, half], S["ra"].at[axis, way, k - 1, half],
                    "rs", (axis, way, k - 1, h), along("yz"[axis], sign + 8))

    norm_products(0)
    rs_round(0, 0)
    norm_products(1)
    yield "dpgather"
    rs_round(0, 1)
    pg, act = (
        jnp.concatenate([S["comb"][h, :, arr].reshape(H, 512) for h in both], axis=1) for arr in (1, 0))
    high = S["u"][...].astype(bf16)
    low = (S["u"][...] - high.astype(f32)).astype(bf16)
    first = jnp.dot(high, pg, preferred_element_type=f32) + jnp.dot(low, pg, preferred_element_type=f32)
    for i in range(8):
        S["s2p"][i, 0:1] = first[0:1, 128 * i:128 * (i + 1)]
    s2a = spread("s2r", d, 4, "dp", lambda i: S["s2p"].at[(d + i) % 8])
    S["s2r"][d] = S["s2p"][d]
    rs_round(1, 0)
    rs_round(1, 1)
    nt_all = jnp.concatenate([S["nt"][i].reshape(K, 128) for i in range(8)], axis=1)
    S["w1g"][...] = lax.dot_general(nt_all, pg, (((1,), (1,)), ((), ())), preferred_element_type=f32)
    store1 = pltpu.make_async_copy(S["w1g"], w1g_hbm, S["loc"].at[2])
    store1.start()
    ends.append(store1.wait)
    arrive(s2a)
    S["s2y"][y] = jnp.sum(S["s2r"][...], axis=0)
    s2b = spread("s2y", y, 5, "y")
    rs_round(2, 0)
    rs_round(2, 1)
    tg_all = jnp.concatenate([S["tg"][i].reshape(K, 128) for i in range(8)], axis=1)
    S["w2g"][...] = lax.dot_general(act, tg_all, (((1,), (1,)), ((), ())), preferred_element_type=f32)
    store2 = pltpu.make_async_copy(S["w2g"], w2g_hbm, S["loc"].at[3])
    store2.start()
    ends.append(store2.wait)
    arrive(s2b)
    S["s2z"][z] = jnp.sum(S["s2y"][...], axis=0)
    s2c = spread("s2z", z, 6, "z")
    rs_round(3, 0)
    rs_round(3, 1)
    arrive(s2c)
    for axis in both:
        for h in both:
            val = rs_block(axis, y if axis == 0 else z, h)
            for way in both:
                val = rs_add(axis, way, 4, h, val)
            S["ng"][pl.ds(4 * h, 4), y if axis == 0 else z, HALF * axis:HALF * (axis + 1)] = val
            S["fs"][pl.ds(4 * h, 4), axis] = val.astype(bf16)
    yield "rings"

    S["ft"][d] = S["fs"][d]
    blocks = spread("ft", d, 7, "dp", lambda i: S["fs"].at[(d + i) % 8])
    for axis, piece in ((0, y), (1, z)):
        rows = slice(HALF * axis, HALF * (axis + 1))
        total = jnp.zeros((HALF, 128), f32)
        for i in range(8):
            mean, inv = scale_of(S["stc"][i])
            total += S["ng"][i, piece, rows] * ((S["xg"][i, piece, rows].astype(f32) - mean) * inv)
        S["pad"][rows] = total
    S["gs"][d] = jnp.broadcast_to(jnp.sum(S["pad"][...].T, axis=0, keepdims=True), (8, 128))
    gains = spread("gs", d, 8, "dp")

    def deliver(number, axis, source, into):
        for i in range(8):
            block = (z + i) % 8
            dev, slot = (at(d, block, y), z) if axis == 0 else (at(d, block, z), y)
            def send():
                return pltpu.make_async_remote_copy(
                    src_ref=source(block), dst_ref=into.at[axis, slot],
                    send_sem=S["fin"].at[0, number if i else 4 + number // 2], recv_sem=S["fin"].at[1, number],
                    device_id=dev, device_id_type=MESH)

            def stay():
                pltpu.make_async_copy(source(block), into.at[axis, slot], S["fin"].at[1, number]).start()

            if i:
                send().start()
            elif axis == 0:
                stay()
            else:
                pl.when(y != z)(lambda: send().start())
                pl.when(y == z)(stay)
                ends.append(functools.partial(when_wait, y != z, send()))
        ends.append(whole(into.at[axis, pl.ds(0, 7)], S["fin"].at[0, number], S["fin"].at[1, number]).wait_send)

    arrive(blocks)
    for axis in both:
        deliver(axis, axis, lambda block: S["ft"].at[block, axis], S["fr"])
    arrive(gains)
    for axis in both:
        deliver(2 + axis, axis, lambda block: S["gs"].at[block], S["gr"])
    gcol = turned(S["gown"][0:1])[:F]
    mean, inv = scale_of(S["stc"][d])
    cen = (x_ref[...].astype(f32) - mean) * inv
    tile = jnp.sum(S["s2z"][...], axis=0)
    base = t_ref[...].astype(f32) - inv * (tile[0:1] / D + cen * (tile[1:2] / D))
    for axis in both:
        whole(S["fr"].at[axis], S["fin"].at[0, axis], S["fin"].at[1, axis]).wait_recv()
    grad = jnp.concatenate([jnp.sum(S["fr"][axis].astype(f32), axis=0) for axis in both], axis=0)
    ig_ref[...] = (base + inv * (grad * gcol)).astype(bf16)
    for axis in both:
        whole(S["gr"].at[axis], S["fin"].at[0, 2 + axis], S["fin"].at[1, 2 + axis]).wait_recv()
    lane = lax.broadcasted_iota(jnp.int32, (8, 128), 1)
    gg_out[...] = jnp.where(lane < HALF, jnp.sum(S["gr"][0], axis=0), jnp.sum(S["gr"][1], axis=0))


def shards(inputs, gain, w_in, w_out, targets):
    vmem, hbm = pl.BlockSpec(memory_space=pltpu.VMEM), pl.BlockSpec(memory_space=pl.ANY)
    scratch = [pltpu.VMEM(shape, kind) for shape, kind in SCRATCH.values()]
    scratch += [pltpu.SemaphoreType.DMA(shape) for shape in SEMS.values()]
    input_grad, gain_grad, w_in_grad, w_out_grad = pl.pallas_call(
        kernel,
        out_shape=(
            jax.ShapeDtypeStruct((F, 128), bf16), jax.ShapeDtypeStruct((8, 128), f32),
            jax.ShapeDtypeStruct((K, H), f32), jax.ShapeDtypeStruct((H, K), f32)),
        in_specs=[vmem, vmem, vmem, hbm, hbm],
        out_specs=(vmem, vmem, hbm, hbm),
        scratch_shapes=scratch,
        compiler_params=pltpu.CompilerParams(
            collective_id=0, has_side_effects=True, vmem_limit_bytes=60 * 1024 * 1024),
        cost_estimate=pl.CostEstimate(flops=2 * 10 ** 9, bytes_accessed=4 * 10 ** 6, transcendentals=10 ** 5),
        name="backward",
    )(inputs.T, targets.T, gain.reshape(1, F), w_in, w_out)
    return input_grad.T, gain_grad[0, :F], w_in_grad, w_out_grad


def solution(mesh):
    return jax.shard_map(
        shards,
        mesh=mesh,
        in_specs=(P("dp", "mp"), P("mp"), P("dp", "mp"), P("mp", "dp"), P("dp", "mp")),
        out_specs=(P("dp", "mp"), P("mp"), P("dp", "mp"), P("mp", "dp")),
        check_vma=False,
    )
```

```python
import functools

import jax
import jax.numpy as jnp
from jax import lax
from jax.experimental import pallas as pl
from jax.experimental.pallas import tpu as pltpu
from jax.sharding import PartitionSpec as P

epsilon = 1e-06
MESH = pl.DeviceIdType.MESH
bf16, f32 = jnp.bfloat16, jnp.float32
D = 6144
F = 96
K = 768
H = 256
Q = 32
HALF = F // 2


def gelu_parts(values):
    cumul = 0.5 * (1.0 + lax.erf(values * 0.7071067811865476))
    slope = cumul + values * jnp.exp(-0.5 * values * values) * 0.3989422804014327
    return values * cumul, slope


def turned(rows):
    return jnp.broadcast_to(rows, (128, 128)).T


SCRATCH = dict(
    w1=((K, H), bf16), w2=((H, K), bf16),
    pad=((128, 128), f32), gown=((8, 128), f32),
    xg=((8, 8, F, 128), bf16), tg=((8, 8, F, 128), bf16), nt=((8, 8, F, 128), bf16),
    gg=((8, 8, 128), f32), gb=((8, F, 128), f32),
    sta=((8, 8, 128), f32), stb=((8, 8, 128), f32), stc=((8, 8, 128), f32),
    part=((2, 2, 4, 2, Q, 512), f32), cs=((2, 4, 2, Q, 512), bf16), cr=((2, 4, 2, Q, 512), bf16),
    xs=((2, 3, 2, Q, 512), bf16), xr=((2, 3, 2, Q, 512), bf16), comb=((2, 8, 2, Q, 512), bf16),
    u=((8, H), f32), s2p=((8, 8, 128), f32), s2r=((8, 8, 128), f32),
    s2y=((8, 8, 128), f32), s2z=((8, 8, 128), f32),
    ng=((8, 8, F, 128), f32), ra=((2, 2, 4, 8, HALF, 128), bf16), sa=((2, 2, 4, 8, HALF, 128), bf16),
    fs=((8, 2, HALF, 128), bf16), ft=((8, 2, HALF, 128), bf16), fr=((8, 2, HALF, 128), bf16),
    w1g=((K, H), f32), w2g=((H, K), f32), gs=((8, 8, 128), f32), gr=((8, 8, 128), f32),
)
SEMS = dict(
    loc=(4,), perm=(2, 3), sx=(2, 7), stg=(2, 7), small=(2, 11), ring_s=(2, 4), ring_r=(2, 2, 4, 4),
    core=(2, 2, 4), xx=(2, 2, 3), ax=(2, 2, 3), ac=(2, 2, 4), rs=(2, 2, 2, 4, 2),
)


def kernel(*refs):
    ends = []
    for _ in phases(ends, *refs):
        pass
    for end in ends:
        end()


def phases(ends, x_ref, t_ref, g_ref, w1_hbm, w2_hbm, ig_ref, gg_out, w1g_hbm, w2g_hbm, *scratch):
    S = dict(zip(list(SCRATCH) + list(SEMS), scratch, strict=True))
    d, m = lax.axis_index("dp"), lax.axis_index("mp")
    z, y = m // 8, m % 8
    chip, core = d // 2, d % 2
    diag = d == z
    off_diag = jnp.logical_not(diag)

    def at(dp, zz, yy):
        return (dp, zz * 8 + yy)

    def remote(src, dst, sem, index, dev):
        return pltpu.make_async_remote_copy(
            src_ref=src, dst_ref=dst, send_sem=S[sem].at[(0, *index)],
            recv_sem=S[sem].at[(1, *index)], device_id=dev, device_id_type=MESH)

    def whole(ref, send_sem, recv_sem):
        return pltpu.make_async_remote_copy(
            src_ref=ref, dst_ref=ref, send_sem=send_sem, recv_sem=recv_sem,
            device_id=at(z, d, y), device_id_type=MESH)

    def go(src, dst, sem, index, dev):
        copy = remote(src, dst, sem, index, dev)
        copy.start()
        ends.append(copy.wait_send)
        return copy

    def along(axis, i):
        if axis == "dp":
            return at((d + i) % 8, z, y)
        if axis == "z":
            return at(d, (z + i) % 8, y)
        return at(d, z, (y + i) % 8)

    def spread(buf, slot, number, axis, source=None):
        for i in range(1, 8):
            src = S[buf].at[slot] if source is None else source(i)
            remote(src, S[buf].at[slot], "small", (number,), along(axis, i)).start()
        seven = whole(S[buf].at[pl.ds(0, 7)], S["small"].at[0, number], S["small"].at[1, number])
        ends.append(seven.wait_send)
        return [seven]

    def arrive(copies):
        for copy in copies:
            copy.wait_recv()

    load1 = pltpu.make_async_copy(w1_hbm, S["w1"], S["loc"].at[0])
    load2 = pltpu.make_async_copy(w2_hbm, S["w2"], S["loc"].at[1])
    load1.start()
    load2.start()
    loads = [load1.wait, load2.wait]
    ends.extend(loads)

    barrier = pltpu.get_barrier_semaphore()

    def hail(dev):
        pl.semaphore_signal(barrier, inc=1, device_id=dev, device_id_type=MESH)

    for axis in ("dp", "z", "y"):
        for i in range(1, 8):
            hail(along(axis, i))

    @pl.when(off_diag)
    def _():
        hail(at(z, d, y))

    S["pad"][...] = jnp.zeros_like(S["pad"])
    S["gown"][...] = jnp.zeros_like(S["gown"])
    S["gown"][:, :F] = jnp.broadcast_to(g_ref[...].astype(f32), (8, F))

    @pl.when(off_diag)
    def _():
        pl.semaphore_wait(barrier, 22)

    @pl.when(diag)
    def _():
        pl.semaphore_wait(barrier, 21)

    yield "barrier"
    perm = [
        (x_ref, S["xg"].at[d, y]),
        (t_ref, S["tg"].at[d, y]),
        (S["gown"], S["gg"].at[y]),
    ]
    perm = [remote(src, dst, "perm", (i,), at(z, d, y)) for i, (src, dst) in enumerate(perm)]

    @pl.when(off_diag)
    def _():
        for copy in perm:
            copy.start()

    @pl.when(diag)
    def _():
        pltpu.make_async_copy(x_ref, S["xg"].at[z, y], S["perm"].at[1, 0]).start()
        pltpu.make_async_copy(t_ref, S["tg"].at[z, y], S["perm"].at[1, 1]).start()
        pltpu.make_async_copy(S["gown"], S["gg"].at[y], S["perm"].at[1, 2]).start()

    @ends.append
    def _():
        @pl.when(off_diag)
        def _():
            for copy in perm:
                copy.wait_send()

    arrive(perm)
    yield "permute"

    gx = [
        go(S["xg"].at[z, y], S["xg"].at[z, y], "sx", (i - 1,), along("z", i)) for i in range(1, 8)]
    gt = [go(S["tg"].at[z, y], S["tg"].at[z, y], "stg", (i - 1,), along("y", i)) for i in range(1, 8)]
    ggain = spread("gg", y, 0, "y")
    piece = S["xg"][z, y].astype(f32)
    S["sta"][y] = jnp.zeros((8, 128), f32)
    S["sta"][y, 0:1] = jnp.sum(piece, axis=0, keepdims=True)
    S["sta"][y, 1:2] = jnp.sum(piece * piece, axis=0, keepdims=True)
    sta = spread("sta", y, 1, "y")
    def offset(e):
        return (e + 1) // 2 if e % 2 else (8 - e // 2) % 8

    def ring_piece(axis, origin, e):
        if isinstance(e, int):
            off = offset(e)
        else:
            off = jnp.where(e % 2 == 1, (e + 1) // 2, (8 - e // 2) % 8)
        if axis == 0:
            return S["xg"].at[(z + off) % 8, origin]
        return S["tg"].at[origin, (y + off) % 8]

    def ring_send(axis, way, k, j, p):
        sign = 1 - 2 * way
        ref = ring_piece(axis, ((y if axis == 0 else z) - sign * (k - 1) + 8) % 8, 2 * j + p)
        pltpu.make_async_remote_copy(
            src_ref=ref, dst_ref=ref, send_sem=S["ring_s"].at[axis, k - 1],
            recv_sem=S["ring_r"].at[axis, way, k - 1, j],
            device_id=along("yz"[axis], sign + 8), device_id_type=MESH).start()

    def ring_wait(axis, way, k, j):
        whole(S["xg"].at[0, pl.ds(0, 2)], S["ring_s"].at[axis, 0], S["ring_r"].at[axis, way, k - 1, j]).wait_recv()

    def ring_rest(k, j, carry):
        for axis in (0, 1):
            for way in (0, 1):
                ring_wait(axis, way, k - 1, j)
                for p in (0, 1):
                    ring_send(axis, way, k, j, p)
        return carry

    def ring_last(j, carry):
        for axis in (0, 1):
            for way in (0, 1):
                ring_wait(axis, way, 3, 2 * j + way)
                for p in (0, 1):
                    ring_send(axis, way, 4, 2 * j + way, p)
        return carry

    for e in range(8):
        for axis in (0, 1):
            if e:
                (gx, gt)[axis][7 - offset(e)].wait_recv()
            for way in (0, 1):
                ring_send(axis, way, 1, e // 2, e % 2)
    for axis in (0, 1):
        for k in (1, 2, 3, 4):
            ends.append(whole(
                S["xg"].at[pl.ds(0, 2)] if k < 4 else S["xg"].at[0],
                S["ring_s"].at[axis, k - 1], S["ring_r"].at[axis, 0, 0, 0]).wait_send)
    yield "ring1"
    arrive(sta)
    S["stb"][d] = jnp.sum(S["sta"][...], axis=0)
    stb = spread("stb", d, 2, "dp")
    arrive(ggain)
    for load in loads:
        load()
        ends.remove(load)
    total = jnp.zeros((8, H), f32)
    for i in range(8):
        rows = S["gg"][i]
        S["gb"][i] = turned(rows[0:1])[:F]
        total += jnp.dot(rows[:, :F].astype(bf16), S["w1"][F * i:F * (i + 1)], preferred_element_type=f32)
    S["u"][...] = total
    lax.fori_loop(0, 4, functools.partial(ring_rest, 2), 0)
    yield "ring2"
    arrive(stb)
    S["stc"][z] = jnp.sum(S["stb"][...], axis=0)
    stc = spread("stc", z, 3, "z")
    lax.fori_loop(0, 4, functools.partial(ring_rest, 3), 0)
    yield "ring3"
    arrive(stc)
    lax.fori_loop(0, 2, ring_last, 0)
    for axis in (0, 1):
        for way in (0, 1):
            for j in (0, 1):
                ring_wait(axis, way, 3, 2 * j + 1 - way)
                ring_wait(axis, way, 4, 2 * j + way)
    yield "ring"

    def scale_of(tile):
        mean = tile[0:1] / D
        return mean, lax.rsqrt(tile[1:2] / D - mean * mean + epsilon)

    def normed(tok, carry):
        mean, inv = scale_of(S["stc"][tok])
        for i in range(8):
            S["nt"][tok, i] = ((S["xg"][tok, i].astype(f32) - mean) * inv * S["gb"][i]).astype(bf16)
        return carry

    lax.fori_loop(0, 8, normed, 0)

    def pair(ref, i):
        return jnp.concatenate(
            [ref[2 * i].reshape(K, 128), ref[2 * i + 1].reshape(K, 128)], axis=1)

    def products(h):
        for i in (2 * h, 2 * h + 1):
            lanes = slice(256 * (i % 2), 256 * (i % 2 + 1))
            pre_part = lax.dot_general(
                S["w1"][...], pair(S["nt"], i), (((0,), (0,)), ((), ())), preferred_element_type=f32)
            act_part = jnp.dot(S["w2"][...], pair(S["tg"], i), preferred_element_type=f32)
            S["part"][h, 0, :, :, :, lanes] = pre_part.reshape(4, 2, Q, 256)
            S["part"][h, 1, :, :, :, lanes] = act_part.reshape(4, 2, Q, 256)
        pairs = {}
        for i in (1, 2, 3, 0):
            to = (chip + i) % 4
            for arr in range(2):
                S["cs"][h, to, arr] = S["part"][h, arr, to, 1 - core].astype(bf16)
            pairs[i] = go(S["cs"].at[h, to], S["cr"].at[h, to], "core", (h, i), at(2 * chip + 1 - core, z, y))
        return pairs

    def chip_sum(h, pairs):
        hops = []
        for i in (1, 2, 3):
            to = (chip + i) % 4
            pairs[i].wait_recv()
            for arr in range(2):
                S["xs"][h, i - 1, arr] = (
                    S["part"][h, arr, to, core] + S["cr"][h, to, arr].astype(f32)).astype(bf16)
            hops.append(go(S["xs"].at[h, i - 1], S["xr"].at[h, i - 1], "xx", (h, i - 1), at(2 * to + core, z, y)))
        return hops

    def activate(h, pairs, hops):
        pairs[0].wait_recv()
        arrive(hops)
        pre_act, act_grad = (
            S["part"][h, arr, chip, core] + S["cr"][h, chip, arr].astype(f32)
            + sum(S["xr"][h, i, arr].astype(f32) for i in range(3)) for arr in range(2))
        value, slope = gelu_parts(pre_act)
        pre_grad = (act_grad * slope).astype(bf16)
        S["comb"][h, d, 0] = value.astype(bf16)
        S["comb"][h, d, 1] = pre_grad
        hops = {
            i: go(S["comb"].at[h, d], S["comb"].at[h, d], "ax", (h, i - 1), at(2 * ((chip + i) % 4) + core, z, y))
            for i in (1, 2, 3)}
        second = jnp.sum(pre_grad.astype(f32) * pre_act, axis=0, keepdims=True)
        for i in range(4):
            S["s2p"][4 * h + i] = jnp.zeros((8, 128), f32)
            S["s2p"][4 * h + i, 1:2] = second[:, 128 * i:128 * (i + 1)]
        return hops

    def pass_on(h, hops):
        pairs = []
        for i in (0, 3, 1, 2):
            slot = 2 * ((chip - i + 4) % 4) + core
            if i:
                hops[i].wait_recv()
            ref = S["comb"].at[h, slot]
            pairs.append(go(ref, ref, "ac", (h, i), at(2 * chip + 1 - core, z, y)))
        return pairs

    both = (0, 1)
    pairs = [products(h) for h in both]
    yield "products"
    hops = [chip_sum(h, pairs[h]) for h in both]
    yield "chipsum"
    hops = [activate(h, pairs[h], hops[h]) for h in both]
    yield "dpsum"
    pairs = [pass_on(h, hops[h]) for h in both]

    def norm_products(h):
        arrive(pairs[h])
        for i in (2 * h, 2 * h + 1):
            lanes = slice(256 * (i % 2), 256 * (i % 2 + 1))
            out = jnp.dot(
                S["w1"][...], S["comb"][h, :, 1, :, lanes].reshape(H, 256), preferred_element_type=f32)
            S["ng"][2 * i] = out[:, :128].reshape(8, F, 128)
            S["ng"][2 * i + 1] = out[:, 128:].reshape(8, F, 128)

    rs = {}

    def rs_block(axis, dest, h):
        return S["ng"][pl.ds(4 * h, 4), dest, HALF * axis:HALF * (axis + 1)]

    def rs_add(axis, way, k, h, val):
        if (axis, way, k, h) in rs:
            rs[axis, way, k, h].wait_recv()
            val = val + S["ra"][axis, way, k - 1, pl.ds(4 * h, 4)].astype(f32)
        return val

    def rs_round(r, h):
        for axis in both:
            for way in both:
                k = r + 1 if h == way else r + 2
                if k > 4:
                    continue
                sign = 1 - 2 * way
                val = rs_block(axis, (y + sign * (5 - k) + 8) % 8, h)
                val = rs_add(axis, way, k - 1, h, val)
                half = pl.ds(4 * h, 4)
                S["sa"][axis, way, k - 1, half] = val.astype(bf16)
                rs[axis, way, k, h] = go(
                    S["sa"].at[axis, way, k - 1, half], S["ra"].at[axis, way, k - 1, half],
                    "rs", (axis, way, k - 1, h), along("y", sign + 8))

    yield "passon"
    norm_products(0)
    rs_round(0, 0)
    norm_products(1)
    yield "dpgather"
    rs_round(0, 1)
    pg, act = (
        jnp.concatenate([S["comb"][h, :, arr].reshape(H, 512) for h in both], axis=1) for arr in (1, 0))
    high = S["u"][...].astype(bf16)
    low = (S["u"][...] - high.astype(f32)).astype(bf16)
    first = jnp.dot(high, pg, preferred_element_type=f32) + jnp.dot(low, pg, preferred_element_type=f32)
    for i in range(8):
        S["s2p"][i, 0:1] = first[0:1, 128 * i:128 * (i + 1)]
    s2a = spread("s2r", d, 4, "dp", lambda i: S["s2p"].at[(d + i) % 8])
    S["s2r"][d] = S["s2p"][d]
    rs_round(1, 0)
    rs_round(1, 1)
    yield "round1"
    nt_all = jnp.concatenate([S["nt"][i].reshape(K, 128) for i in range(8)], axis=1)
    S["w1g"][...] = lax.dot_general(nt_all, pg, (((1,), (1,)), ((), ())), preferred_element_type=f32)
    store1 = pltpu.make_async_copy(S["w1g"], w1g_hbm, S["loc"].at[2])
    store1.start()
    ends.append(store1.wait)
    yield "w1g"
    arrive(s2a)
    S["s2y"][y] = jnp.sum(S["s2r"][...], axis=0)
    s2b = spread("s2y", y, 5, "y")
    rs_round(2, 0)
    rs_round(2, 1)
    yield "round2"
    tg_all = jnp.concatenate([S["tg"][i].reshape(K, 128) for i in range(8)], axis=1)
    S["w2g"][...] = lax.dot_general(act, tg_all, (((1,), (1,)), ((), ())), preferred_element_type=f32)
    store2 = pltpu.make_async_copy(S["w2g"], w2g_hbm, S["loc"].at[3])
    store2.start()
    ends.append(store2.wait)
    yield "w2g"
    arrive(s2b)
    S["s2z"][z] = jnp.sum(S["s2y"][...], axis=0)
    s2c = spread("s2z", z, 6, "z")
    rs_round(3, 0)
    rs_round(3, 1)
    yield "round3"
    arrive(s2c)
    for axis in both:
        for h in both:
            val = rs_block(axis, y, h)
            for way in both:
                val = rs_add(axis, way, 4, h, val)
            S["ng"][pl.ds(4 * h, 4), y, HALF * axis:HALF * (axis + 1)] = val
            S["fs"][pl.ds(4 * h, 4), axis] = val.astype(bf16)
    yield "rings"

    S["ft"][d] = S["fs"][d]
    blocks = spread("ft", d, 7, "dp", lambda i: S["fs"].at[(d + i) % 8])
    total = jnp.zeros((F, 128), f32)
    for i in range(8):
        mean, inv = scale_of(S["stc"][i])
        total += S["ng"][i, y] * ((S["xg"][i, y].astype(f32) - mean) * inv)
    S["pad"][:F] = total
    S["gs"][d] = jnp.broadcast_to(jnp.sum(S["pad"][...].T, axis=0, keepdims=True), (8, 128))
    gains = spread("gs", d, 8, "dp")

    yield "gainsum"
    arrive(blocks)
    S["fr"][z] = S["ft"][z]
    owned = spread("fr", z, 9, "z", lambda i: S["ft"].at[(z + i) % 8])
    yield "deliver1"
    arrive(gains)
    S["gr"][z] = S["gs"][z]
    gain_parts = spread("gr", z, 10, "z", lambda i: S["gs"].at[(z + i) % 8])
    yield "deliver2"
    gcol = turned(S["gown"][0:1])[:F]
    mean, inv = scale_of(S["stc"][d])
    cen = (x_ref[...].astype(f32) - mean) * inv
    tile = jnp.sum(S["s2z"][...], axis=0)
    base = t_ref[...].astype(f32) - inv * (tile[0:1] / D + cen * (tile[1:2] / D))
    arrive(owned)
    grad = jnp.sum(S["fr"][...].astype(f32), axis=0).reshape(F, 128)
    ig_ref[...] = (base + inv * (grad * gcol)).astype(bf16)
    arrive(gain_parts)
    yield "final"
    gg_out[...] = jnp.sum(S["gr"][...], axis=0)


def hand_over(*refs):
    ins, outs, sem = refs[:4], refs[4:8], refs[8]
    copies = [pltpu.make_async_copy(ins[i], outs[i], sem.at[i]) for i in (0, 1)]
    for copy in copies:
        copy.start()
    outs[2][...] = ins[2][...]
    outs[3][...] = ins[3][0:1, :F]
    for copy in copies:
        copy.wait()


def shards(inputs, gain, w_in, w_out, targets):
    vmem, hbm = pl.BlockSpec(memory_space=pltpu.VMEM), pl.BlockSpec(memory_space=pl.ANY)
    scratch = [pltpu.VMEM(shape, kind) for shape, kind in SCRATCH.values()]
    scratch += [pltpu.SemaphoreType.DMA(shape) for shape in SEMS.values()]
    input_grad, gain_grad, w_in_grad, w_out_grad = pl.pallas_call(
        kernel,
        out_shape=(
            jax.ShapeDtypeStruct((F, 128), bf16), jax.ShapeDtypeStruct((8, 128), f32),
            jax.ShapeDtypeStruct((K, H), f32), jax.ShapeDtypeStruct((H, K), f32)),
        in_specs=[vmem, vmem, vmem, hbm, hbm],
        out_specs=(vmem, vmem, hbm, hbm),
        scratch_shapes=scratch,
        compiler_params=pltpu.CompilerParams(
            collective_id=0, has_side_effects=True, vmem_limit_bytes=60 * 1024 * 1024),
        cost_estimate=pl.CostEstimate(flops=2 * 10 ** 9, bytes_accessed=4 * 10 ** 6, transcendentals=10 ** 5),
        name="backward",
    )(inputs.T, targets.T, gain.reshape(1, F), w_in, w_out)
    w_in_grad, w_out_grad, input_grad, gain_grad = pl.pallas_call(
        hand_over,
        out_shape=(
            jax.ShapeDtypeStruct((K, H), f32), jax.ShapeDtypeStruct((H, K), f32),
            jax.ShapeDtypeStruct((F, 128), bf16), jax.ShapeDtypeStruct((1, F), f32)),
        in_specs=[hbm, hbm, vmem, vmem],
        out_specs=(hbm, hbm, vmem, vmem),
        scratch_shapes=[pltpu.SemaphoreType.DMA((2,))],
        compiler_params=pltpu.CompilerParams(vmem_limit_bytes=60 * 1024 * 1024),
        cost_estimate=pl.CostEstimate(flops=0, bytes_accessed=3 * 10 ** 6, transcendentals=0),
        name="hand_over",
    )(w_in_grad, w_out_grad, input_grad, gain_grad)
    return input_grad.T, gain_grad.reshape(F), w_in_grad, w_out_grad


def solution(mesh):
    return jax.shard_map(
        shards,
        mesh=mesh,
        in_specs=(P("dp", "mp"), P("mp"), P("dp", "mp"), P("mp", "dp"), P("dp", "mp")),
        out_specs=(P("dp", "mp"), P("mp"), P("dp", "mp"), P("mp", "dp")),
        check_vma=False,
    )
```

```python
import functools

import jax
import jax.numpy as jnp
from jax import lax
from jax.experimental import pallas as pl
from jax.experimental.pallas import tpu as pltpu
from jax.sharding import PartitionSpec as P

epsilon = 1e-06
MESH = pl.DeviceIdType.MESH
bf16, f32 = jnp.bfloat16, jnp.float32
D = 6144
F = 96
K = 768
H = 256
Q = 32
HALF = F // 2


def gelu_parts(values):
    cumul = 0.5 * (1.0 + lax.erf(values * 0.7071067811865476))
    slope = cumul + values * jnp.exp(-0.5 * values * values) * 0.3989422804014327
    return values * cumul, slope


def turned(rows):
    return jnp.broadcast_to(rows, (128, 128)).T


SCRATCH = dict(
    w1=((K, H), bf16), w2=((H, K), bf16),
    pad=((128, 128), f32), gown=((8, 128), f32),
    xg=((8, 8, F, 128), bf16), tg=((8, 8, F, 128), bf16), nt=((8, 8, F, 128), bf16),
    gg=((8, 8, 128), f32), gb=((8, F, 128), f32),
    sta=((8, 8, 128), f32), stb=((8, 8, 128), f32), stc=((8, 8, 128), f32),
    part=((2, 2, 4, 2, Q, 512), f32), cs=((2, 4, 2, Q, 512), bf16), cr=((2, 4, 2, Q, 512), bf16),
    xs=((2, 3, 2, Q, 512), bf16), xr=((2, 3, 2, Q, 512), bf16), comb=((2, 8, 2, Q, 512), bf16),
    u=((8, H), f32), s2p=((8, 8, 128), f32), s2r=((8, 8, 128), f32),
    s2y=((8, 8, 128), f32), s2z=((8, 8, 128), f32),
    ng=((8, 8, F, 128), f32), ra=((2, 2, 4, 8, HALF, 128), bf16), sa=((2, 2, 4, 8, HALF, 128), bf16),
    fs=((8, 2, HALF, 128), bf16), ft=((8, 2, HALF, 128), bf16), fr=((8, 2, HALF, 128), bf16),
    w1g=((K, H), f32), w2g=((H, K), f32), gs=((8, 8, 128), f32), gr=((8, 8, 128), f32),
)
SEMS = dict(
    loc=(4,), perm=(2, 3), sx=(2, 7), stg=(2, 7), small=(2, 11), ring_s=(2, 4), ring_r=(2, 2, 4, 4),
    core=(2, 2, 4), xx=(2, 2, 3), ax=(2, 2, 3), ac=(2, 2, 4), rs=(2, 2, 2, 4, 2),
)


def kernel(*refs):
    ends = []
    for _ in phases(ends, *refs):
        pass
    for end in ends:
        end()


def phases(ends, x_ref, t_ref, g_ref, w1_hbm, w2_hbm, ig_ref, gg_out, w1g_hbm, w2g_hbm, *scratch):
    S = dict(zip(list(SCRATCH) + list(SEMS), scratch, strict=True))
    d, m = lax.axis_index("dp"), lax.axis_index("mp")
    z, y = m // 8, m % 8
    chip, core = d // 2, d % 2
    diag = d == z
    off_diag = jnp.logical_not(diag)

    def at(dp, zz, yy):
        return (dp, zz * 8 + yy)

    def remote(src, dst, sem, index, dev):
        return pltpu.make_async_remote_copy(
            src_ref=src, dst_ref=dst, send_sem=S[sem].at[(0, *index)],
            recv_sem=S[sem].at[(1, *index)], device_id=dev, device_id_type=MESH)

    def whole(ref, send_sem, recv_sem):
        return pltpu.make_async_remote_copy(
            src_ref=ref, dst_ref=ref, send_sem=send_sem, recv_sem=recv_sem,
            device_id=at(z, d, y), device_id_type=MESH)

    def go(src, dst, sem, index, dev):
        copy = remote(src, dst, sem, index, dev)
        copy.start()
        ends.append(copy.wait_send)
        return copy

    def along(axis, i):
        if axis == "dp":
            return at((d + i) % 8, z, y)
        if axis == "z":
            return at(d, (z + i) % 8, y)
        return at(d, z, (y + i) % 8)

    def spread(buf, slot, number, axis, source=None):
        for i in range(1, 8):
            src = S[buf].at[slot] if source is None else source(i)
            remote(src, S[buf].at[slot], "small", (number,), along(axis, i)).start()
        seven = whole(S[buf].at[pl.ds(0, 7)], S["small"].at[0, number], S["small"].at[1, number])
        ends.append(seven.wait_send)
        return [seven]

    def arrive(copies):
        for copy in copies:
            copy.wait_recv()

    load1 = pltpu.make_async_copy(w1_hbm, S["w1"], S["loc"].at[0])
    load2 = pltpu.make_async_copy(w2_hbm, S["w2"], S["loc"].at[1])
    load1.start()
    load2.start()
    loads = [load1.wait, load2.wait]
    ends.extend(loads)

    barrier = pltpu.get_barrier_semaphore()

    def hail(dev):
        pl.semaphore_signal(barrier, inc=1, device_id=dev, device_id_type=MESH)

    for axis in ("dp", "z", "y"):
        for i in range(1, 8):
            hail(along(axis, i))

    @pl.when(off_diag)
    def _():
        hail(at(z, d, y))

    S["pad"][...] = jnp.zeros_like(S["pad"])
    S["gown"][...] = jnp.zeros_like(S["gown"])
    S["gown"][:, :F] = jnp.broadcast_to(g_ref[...].astype(f32), (8, F))

    @pl.when(off_diag)
    def _():
        pl.semaphore_wait(barrier, 22)

    @pl.when(diag)
    def _():
        pl.semaphore_wait(barrier, 21)

    yield "barrier"
    perm = [
        (x_ref, S["xg"].at[d, y]),
        (t_ref, S["tg"].at[d, y]),
        (S["gown"], S["gg"].at[y]),
    ]
    perm = [remote(src, dst, "perm", (i,), at(z, d, y)) for i, (src, dst) in enumerate(perm)]

    @pl.when(off_diag)
    def _():
        for copy in perm:
            copy.start()

    @pl.when(diag)
    def _():
        pltpu.make_async_copy(x_ref, S["xg"].at[z, y], S["perm"].at[1, 0]).start()
        pltpu.make_async_copy(t_ref, S["tg"].at[z, y], S["perm"].at[1, 1]).start()
        pltpu.make_async_copy(S["gown"], S["gg"].at[y], S["perm"].at[1, 2]).start()

    @ends.append
    def _():
        @pl.when(off_diag)
        def _():
            for copy in perm:
                copy.wait_send()

    arrive(perm)
    yield "permute"

    ggain = spread("gg", y, 0, "y")
    piece = S["xg"][z, y].astype(f32)
    S["sta"][y] = jnp.zeros((8, 128), f32)
    S["sta"][y, 0:1] = jnp.sum(piece, axis=0, keepdims=True)
    S["sta"][y, 1:2] = jnp.sum(piece * piece, axis=0, keepdims=True)
    sta = spread("sta", y, 1, "y")

    gx = [
        go(S["xg"].at[z, y], S["xg"].at[z, y], "sx", (i - 1,), along("z", i)) for i in range(1, 8)]
    gt = [go(S["tg"].at[z, y], S["tg"].at[z, y], "stg", (i - 1,), along("y", i)) for i in range(1, 8)]
    def offset(e):
        return (e + 1) // 2 if e % 2 else (8 - e // 2) % 8

    def ring_piece(axis, origin, e):
        if isinstance(e, int):
            off = offset(e)
        else:
            off = jnp.where(e % 2 == 1, (e + 1) // 2, (8 - e // 2) % 8)
        if axis == 0:
            return S["xg"].at[(z + off) % 8, origin]
        return S["tg"].at[origin, (y + off) % 8]

    def ring_send(axis, way, k, j, p):
        sign = 1 - 2 * way
        ref = ring_piece(axis, ((y if axis == 0 else z) - sign * (k - 1) + 8) % 8, 2 * j + p)
        pltpu.make_async_remote_copy(
            src_ref=ref, dst_ref=ref, send_sem=S["ring_s"].at[axis, k - 1],
            recv_sem=S["ring_r"].at[axis, way, k - 1, j],
            device_id=along("yz"[axis], sign + 8), device_id_type=MESH).start()

    def ring_wait(axis, way, k, j):
        whole(S["xg"].at[0, pl.ds(0, 2)], S["ring_s"].at[axis, 0], S["ring_r"].at[axis, way, k - 1, j]).wait_recv()

    def ring_rest(k, j, carry):
        for axis in (0, 1):
            for way in (0, 1):
                ring_wait(axis, way, k - 1, j)
                for p in (0, 1):
                    ring_send(axis, way, k, j, p)
        return carry

    def ring_last(j, carry):
        for axis in (0, 1):
            for way in (0, 1):
                ring_wait(axis, way, 3, 2 * j + way)
                for p in (0, 1):
                    ring_send(axis, way, 4, 2 * j + way, p)
        return carry

    for e in range(8):
        for axis in (0, 1):
            if e:
                (gx, gt)[axis][7 - offset(e)].wait_recv()
            for way in (0, 1):
                ring_send(axis, way, 1, e // 2, e % 2)
    for axis in (0, 1):
        for k in (1, 2, 3, 4):
            ends.append(whole(
                S["xg"].at[pl.ds(0, 2)] if k < 4 else S["xg"].at[0],
                S["ring_s"].at[axis, k - 1], S["ring_r"].at[axis, 0, 0, 0]).wait_send)
    yield "ring1"
    arrive(sta)
    S["stb"][d] = jnp.sum(S["sta"][...], axis=0)
    stb = spread("stb", d, 2, "dp")
    lax.fori_loop(0, 4, functools.partial(ring_rest, 2), 0)
    yield "ring2"
    arrive(stb)
    S["stc"][z] = jnp.sum(S["stb"][...], axis=0)
    stc = spread("stc", z, 3, "z")
    lax.fori_loop(0, 4, functools.partial(ring_rest, 3), 0)
    yield "ring3"
    arrive(ggain)
    for load in loads:
        load()
        ends.remove(load)
    total = jnp.zeros((8, H), f32)
    for i in range(8):
        rows = S["gg"][i]
        S["gb"][i] = turned(rows[0:1])[:F]
        total += jnp.dot(rows[:, :F].astype(bf16), S["w1"][F * i:F * (i + 1)], preferred_element_type=f32)
    S["u"][...] = total
    arrive(stc)
    lax.fori_loop(0, 2, ring_last, 0)
    for way in (0, 1):
        ring_wait(0, way, 3, 1 - way)
        ring_wait(0, way, 4, way)
    yield "ringhalf"

    place = [(z + offset(e)) % 8 for e in range(8)]

    def scale_of(tile):
        mean = tile[0:1] / D
        return mean, lax.rsqrt(tile[1:2] / D - mean * mean + epsilon)

    def normed(h):
        for e in range(4 * h, 4 * h + 4):
            mean, inv = scale_of(S["stc"][place[e]])

            def rows(i, carry):
                S["nt"][e, i] = ((S["xg"][place[e], i].astype(f32) - mean) * inv * S["gb"][i]).astype(bf16)
                return carry

            lax.fori_loop(0, 8, rows, 0)

    def joined(ref, spots):
        return jnp.concatenate([ref[i].reshape(K, 128) for i in spots], axis=1)

    def products(h):
        for i in (2 * h, 2 * h + 1):
            lanes = slice(256 * (i % 2), 256 * (i % 2 + 1))
            pre_part = lax.dot_general(
                S["w1"][...], joined(S["nt"], (2 * i, 2 * i + 1)), (((0,), (0,)), ((), ())), preferred_element_type=f32)
            act_part = jnp.dot(S["w2"][...], joined(S["tg"], place[2 * i:2 * i + 2]), preferred_element_type=f32)
            S["part"][h, 0, :, :, :, lanes] = pre_part.reshape(4, 2, Q, 256)
            S["part"][h, 1, :, :, :, lanes] = act_part.reshape(4, 2, Q, 256)
        pairs = {}
        for i in (1, 2, 3, 0):
            to = (chip + i) % 4
            for arr in range(2):
                S["cs"][h, to, arr] = S["part"][h, arr, to, 1 - core].astype(bf16)
            pairs[i] = go(S["cs"].at[h, to], S["cr"].at[h, to], "core", (h, i), at(2 * chip + 1 - core, z, y))
        return pairs

    def chip_sum(h, pairs):
        hops = []
        for i in (1, 2, 3):
            to = (chip + i) % 4
            pairs[i].wait_recv()
            for arr in range(2):
                S["xs"][h, i - 1, arr] = (
                    S["part"][h, arr, to, core] + S["cr"][h, to, arr].astype(f32)).astype(bf16)
            hops.append(go(S["xs"].at[h, i - 1], S["xr"].at[h, i - 1], "xx", (h, i - 1), at(2 * to + core, z, y)))
        return hops

    def activate(h, pairs, hops):
        pairs[0].wait_recv()
        arrive(hops)
        pre_act, act_grad = (
            S["part"][h, arr, chip, core] + S["cr"][h, chip, arr].astype(f32)
            + sum(S["xr"][h, i, arr].astype(f32) for i in range(3)) for arr in range(2))
        value, slope = gelu_parts(pre_act)
        pre_grad = (act_grad * slope).astype(bf16)
        S["comb"][h, d, 0] = value.astype(bf16)
        S["comb"][h, d, 1] = pre_grad
        hops = {
            i: go(S["comb"].at[h, d], S["comb"].at[h, d], "ax", (h, i - 1), at(2 * ((chip + i) % 4) + core, z, y))
            for i in (1, 2, 3)}
        second = jnp.sum(pre_grad.astype(f32) * pre_act, axis=0, keepdims=True)
        for i in range(4):
            S["s2p"][place[4 * h + i]] = jnp.zeros((8, 128), f32)
            S["s2p"][place[4 * h + i], 1:2] = second[:, 128 * i:128 * (i + 1)]
        return hops

    def pass_on(h, hops):
        pairs = []
        for i in (0, 3, 1, 2):
            slot = 2 * ((chip - i + 4) % 4) + core
            if i:
                hops[i].wait_recv()
            ref = S["comb"].at[h, slot]
            pairs.append(go(ref, ref, "ac", (h, i), at(2 * chip + 1 - core, z, y)))
        return pairs

    both = (0, 1)
    normed(0)
    pairs = {0: products(0)}
    hops = {0: chip_sum(0, pairs[0])}
    for way in both:
        ring_wait(0, way, 3, 3 - way)
        ring_wait(0, way, 4, 2 + way)
        for j in both:
            ring_wait(1, way, 3, 2 * j + 1 - way)
            ring_wait(1, way, 4, 2 * j + way)
    normed(1)
    pairs[1] = products(1)
    hops[1] = chip_sum(1, pairs[1])
    yield "chipsum"
    hops = [activate(h, pairs[h], hops[h]) for h in both]
    yield "dpsum"
    pairs = [pass_on(h, hops[h]) for h in both]

    def norm_products(h):
        arrive(pairs[h])
        for i in (2 * h, 2 * h + 1):
            lanes = slice(256 * (i % 2), 256 * (i % 2 + 1))
            out = jnp.dot(
                S["w1"][...], S["comb"][h, :, 1, :, lanes].reshape(H, 256), preferred_element_type=f32)
            S["ng"][2 * i] = out[:, :128].reshape(8, F, 128)
            S["ng"][2 * i + 1] = out[:, 128:].reshape(8, F, 128)

    rs = {}

    def rs_block(axis, dest, h):
        return S["ng"][pl.ds(4 * h, 4), dest, HALF * axis:HALF * (axis + 1)]

    def rs_add(axis, way, k, h, val):
        if (axis, way, k, h) in rs:
            rs[axis, way, k, h].wait_recv()
            val = val + S["ra"][axis, way, k - 1, pl.ds(4 * h, 4)].astype(f32)
        return val

    def rs_round(r, h):
        for axis in both:
            for way in both:
                k = r + 1 if h == way else r + 2
                if k > 4:
                    continue
                sign = 1 - 2 * way
                val = rs_block(axis, (y + sign * (5 - k) + 8) % 8, h)
                val = rs_add(axis, way, k - 1, h, val)
                half = pl.ds(4 * h, 4)
                S["sa"][axis, way, k - 1, half] = val.astype(bf16)
                rs[axis, way, k, h] = go(
                    S["sa"].at[axis, way, k - 1, half], S["ra"].at[axis, way, k - 1, half],
                    "rs", (axis, way, k - 1, h), along("y", sign + 8))

    yield "passon"
    norm_products(0)
    rs_round(0, 0)
    norm_products(1)
    yield "dpgather"
    rs_round(0, 1)
    pg, act = (
        jnp.concatenate([S["comb"][h, :, arr].reshape(H, 512) for h in both], axis=1) for arr in (1, 0))
    high = S["u"][...].astype(bf16)
    low = (S["u"][...] - high.astype(f32)).astype(bf16)
    first = jnp.dot(high, pg, preferred_element_type=f32) + jnp.dot(low, pg, preferred_element_type=f32)
    for i in range(8):
        S["s2p"][place[i], 0:1] = first[0:1, 128 * i:128 * (i + 1)]
    s2a = spread("s2r", d, 4, "dp", lambda i: S["s2p"].at[(d + i) % 8])
    S["s2r"][d] = S["s2p"][d]
    rs_round(1, 0)
    rs_round(1, 1)
    yield "round1"
    nt_all = joined(S["nt"], range(8))
    S["w1g"][...] = lax.dot_general(nt_all, pg, (((1,), (1,)), ((), ())), preferred_element_type=f32)
    store1 = pltpu.make_async_copy(S["w1g"], w1g_hbm, S["loc"].at[2])
    store1.start()
    ends.append(store1.wait)
    yield "w1g"
    arrive(s2a)
    S["s2y"][y] = jnp.sum(S["s2r"][...], axis=0)
    s2b = spread("s2y", y, 5, "y")
    rs_round(2, 0)
    rs_round(2, 1)
    yield "round2"
    tg_all = joined(S["tg"], place)
    S["w2g"][...] = lax.dot_general(act, tg_all, (((1,), (1,)), ((), ())), preferred_element_type=f32)
    store2 = pltpu.make_async_copy(S["w2g"], w2g_hbm, S["loc"].at[3])
    store2.start()
    ends.append(store2.wait)
    yield "w2g"
    arrive(s2b)
    S["s2z"][z] = jnp.sum(S["s2y"][...], axis=0)
    s2c = spread("s2z", z, 6, "z")
    rs_round(3, 0)
    rs_round(3, 1)
    yield "round3"
    arrive(s2c)
    for axis in both:
        for h in both:
            val = rs_block(axis, y, h)
            for way in both:
                val = rs_add(axis, way, 4, h, val)
            for i in range(4):
                S["ng"][4 * h + i, y, HALF * axis:HALF * (axis + 1)] = val[i]
                S["fs"][place[4 * h + i], axis] = val[i].astype(bf16)
    yield "rings"

    S["ft"][d] = S["fs"][d]
    blocks = spread("ft", d, 7, "dp", lambda i: S["fs"].at[(d + i) % 8])
    total = jnp.zeros((F, 128), f32)
    for i in range(8):
        mean, inv = scale_of(S["stc"][place[i]])
        total += S["ng"][i, y] * ((S["xg"][place[i], y].astype(f32) - mean) * inv)
    S["pad"][:F] = total
    S["gs"][d] = jnp.broadcast_to(jnp.sum(S["pad"][...].T, axis=0, keepdims=True), (8, 128))
    gains = spread("gs", d, 8, "dp")

    yield "gainsum"
    arrive(blocks)
    S["fr"][z] = S["ft"][z]
    owned = spread("fr", z, 9, "z", lambda i: S["ft"].at[(z + i) % 8])
    yield "deliver1"
    arrive(gains)
    S["gr"][z] = S["gs"][z]
    gain_parts = spread("gr", z, 10, "z", lambda i: S["gs"].at[(z + i) % 8])
    yield "deliver2"
    gcol = turned(S["gown"][0:1])[:F]
    mean, inv = scale_of(S["stc"][d])
    cen = (x_ref[...].astype(f32) - mean) * inv
    tile = jnp.sum(S["s2z"][...], axis=0)
    base = t_ref[...].astype(f32) - inv * (tile[0:1] / D + cen * (tile[1:2] / D))
    arrive(owned)
    grad = jnp.sum(S["fr"][...].astype(f32), axis=0).reshape(F, 128)
    ig_ref[...] = (base + inv * (grad * gcol)).astype(bf16)
    arrive(gain_parts)
    yield "final"
    gg_out[...] = jnp.sum(S["gr"][...], axis=0)


def hand_over(*refs):
    ins, outs, held, sem = refs[:4], refs[4:8], refs[8:10], refs[10]
    steps = []
    for i in (0, 1):
        rows = ins[i].shape[0] // 4
        for part in range(4):
            span = pl.ds(rows * part, rows)
            steps.append((
                pltpu.make_async_copy(ins[i].at[span], held[i].at[span], sem.at[0, i, part]),
                pltpu.make_async_copy(held[i].at[span], outs[i].at[span], sem.at[1, i, part])))
    for load, _ in steps:
        load.start()
    outs[2][...] = ins[2][...]
    outs[3][...] = ins[3][0:1, :F]
    for load, store in steps:
        load.wait()
        store.start()
    for _, store in steps:
        store.wait()


def shards(inputs, gain, w_in, w_out, targets):
    vmem, hbm = pl.BlockSpec(memory_space=pltpu.VMEM), pl.BlockSpec(memory_space=pl.ANY)
    scratch = [pltpu.VMEM(shape, kind) for shape, kind in SCRATCH.values()]
    scratch += [pltpu.SemaphoreType.DMA(shape) for shape in SEMS.values()]
    input_grad, gain_grad, w_in_grad, w_out_grad = pl.pallas_call(
        kernel,
        out_shape=(
            jax.ShapeDtypeStruct((F, 128), bf16), jax.ShapeDtypeStruct((8, 128), f32),
            jax.ShapeDtypeStruct((K, H), f32), jax.ShapeDtypeStruct((H, K), f32)),
        in_specs=[vmem, vmem, vmem, hbm, hbm],
        out_specs=(vmem, vmem, hbm, hbm),
        scratch_shapes=scratch,
        compiler_params=pltpu.CompilerParams(
            collective_id=0, has_side_effects=True, vmem_limit_bytes=60 * 1024 * 1024),
        cost_estimate=pl.CostEstimate(flops=2 * 10 ** 9, bytes_accessed=4 * 10 ** 6, transcendentals=10 ** 5),
        name="backward",
    )(inputs.T, targets.T, gain.reshape(1, F), w_in, w_out)
    w_in_grad, w_out_grad, input_grad, gain_grad = pl.pallas_call(
        hand_over,
        out_shape=(
            jax.ShapeDtypeStruct((K, H), f32), jax.ShapeDtypeStruct((H, K), f32),
            jax.ShapeDtypeStruct((F, 128), bf16), jax.ShapeDtypeStruct((1, F), f32)),
        in_specs=[hbm, hbm, vmem, vmem],
        out_specs=(hbm, hbm, vmem, vmem),
        scratch_shapes=[
            pltpu.VMEM((K, H), f32), pltpu.VMEM((H, K), f32), pltpu.SemaphoreType.DMA((2, 2, 4))],
        compiler_params=pltpu.CompilerParams(vmem_limit_bytes=60 * 1024 * 1024),
        cost_estimate=pl.CostEstimate(flops=0, bytes_accessed=3 * 10 ** 6, transcendentals=0),
        name="hand_over",
    )(w_in_grad, w_out_grad, input_grad, gain_grad)
    return input_grad.T, gain_grad.reshape(F), w_in_grad, w_out_grad


def solution(mesh):
    return jax.shard_map(
        shards,
        mesh=mesh,
        in_specs=(P("dp", "mp"), P("mp"), P("dp", "mp"), P("mp", "dp"), P("dp", "mp")),
        out_specs=(P("dp", "mp"), P("mp"), P("dp", "mp"), P("mp", "dp")),
        check_vma=False,
    )
```

```python
import functools

import jax
import jax.numpy as jnp
from jax import lax
from jax.experimental import pallas as pl
from jax.experimental.pallas import tpu as pltpu
from jax.sharding import PartitionSpec as P

epsilon = 1e-06
MESH = pl.DeviceIdType.MESH
bf16, f32 = jnp.bfloat16, jnp.float32
D = 6144
F = 96
K = 768
H = 256
Q = 32
HALF = F // 2


def gelu_parts(values):
    cumul = 0.5 * (1.0 + lax.erf(values * 0.7071067811865476))
    slope = cumul + values * jnp.exp(-0.5 * values * values) * 0.3989422804014327
    return values * cumul, slope


def turned(rows):
    return jnp.broadcast_to(rows, (128, 128)).T


SCRATCH = dict(
    w1=((K, H), bf16), w2=((H, K), bf16),
    pad=((128, 128), f32), xo=((F, 128), bf16), to=((F, 128), bf16), go=((1, F), bf16),
    igv=((F, 128), bf16), ggv=((1, F), f32), gown=((8, 128), f32),
    xg=((8, 8, F, 128), bf16), tg=((8, 8, F, 128), bf16), nt=((8, 8, F, 128), bf16),
    gg=((8, 8, 128), f32), gb=((8, F, 128), f32),
    sta=((8, 8, 128), f32), stb=((8, 8, 128), f32), stc=((8, 8, 128), f32),
    part=((2, 2, 4, 2, Q, 512), f32), cs=((2, 4, 2, Q, 512), bf16), cr=((2, 4, 2, Q, 512), bf16),
    xs=((2, 3, 2, Q, 512), bf16), xr=((2, 3, 2, Q, 512), bf16), comb=((2, 8, 2, Q, 512), bf16),
    u=((8, H), f32), s2p=((8, 8, 128), f32), s2r=((8, 8, 128), f32),
    s2y=((8, 8, 128), f32), s2z=((8, 8, 128), f32),
    ng=((8, 8, F, 128), f32), ra=((2, 4, 2, 8, HALF, 128), bf16), sa=((2, 4, 2, 8, HALF, 128), bf16),
    fs=((2, 8, HALF, 128), bf16), ft=((2, 8, HALF, 128), bf16), fr=((2, 8, HALF, 128), bf16),
    w1g=((K, H), f32), w2g=((H, K), f32), gs=((8, 8, 128), f32), gr=((8, 8, 128), f32),
)
SEMS = dict(
    loc=(9,), perm=(2, 3), sx=(8,), stg=(8,), small=(2, 13), ring_s=(2, 4), ring_r=(2, 2, 4, 4),
    core=(2, 2, 4), xx=(2, 2, 3), ax=(2, 2, 3), ac=(2, 2, 4), rs_s=(2, 4), rs_r=(2, 2, 4, 2),
)


def kernel(*refs):
    ends = []
    for _ in phases(ends, *refs):
        pass
    for end in ends:
        end()


def phases(ends, x_hbm, t_hbm, g_hbm, w1_hbm, w2_hbm, ig_hbm, gg_hbm, w1g_hbm, w2g_hbm, *scratch):
    S = dict(zip(list(SCRATCH) + list(SEMS), scratch, strict=True))
    d, m = lax.axis_index("dp"), lax.axis_index("mp")
    z, y = m // 8, m % 8
    chip, core = d // 2, d % 2
    diag = d == z
    off_diag = jnp.logical_not(diag)

    def at(dp, zz, yy):
        return (dp, zz * 8 + yy)

    def remote(src, dst, sem, index, dev):
        return pltpu.make_async_remote_copy(
            src_ref=src, dst_ref=dst, send_sem=S[sem].at[(0, *index)],
            recv_sem=S[sem].at[(1, *index)], device_id=dev, device_id_type=MESH)

    def whole(ref, send_sem, recv_sem):
        return pltpu.make_async_remote_copy(
            src_ref=ref, dst_ref=ref, send_sem=send_sem, recv_sem=recv_sem,
            device_id=at(z, d, y), device_id_type=MESH)

    def go(src, dst, sem, index, dev):
        copy = remote(src, dst, sem, index, dev)
        copy.start()
        ends.append(copy.wait_send)
        return copy

    def along(axis, i):
        if axis == "dp":
            return at((d + i) % 8, z, y)
        if axis == "z":
            return at(d, (z + i) % 8, y)
        return at(d, z, (y + i) % 8)

    def scatter(ref, slot, number, axis, source=None):
        for i in range(1, 8):
            src = ref.at[slot] if source is None else source(i)
            remote(src, ref.at[slot], "small", (number,), along(axis, i)).start()
        seven = whole(ref.at[pl.ds(0, 7)], S["small"].at[0, number], S["small"].at[1, number])
        ends.append(seven.wait_send)
        return [seven]

    def spread(buf, *rest):
        return scatter(S[buf], *rest)

    def arrive(copies):
        for copy in copies:
            copy.wait_recv()

    def local(src, dst, number):
        copy = pltpu.make_async_copy(src, dst, S["loc"].at[number])
        copy.start()
        return copy

    small_loads = [local(ref, S[name], i) for i, (ref, name) in enumerate(((x_hbm, "xo"), (t_hbm, "to"), (g_hbm, "go")))]
    loads = [local(w1_hbm, S["w1"], 3).wait, local(w2_hbm, S["w2"], 4).wait]
    ends.extend(loads)

    barrier = pltpu.get_barrier_semaphore()

    def hail(dev):
        pl.semaphore_signal(barrier, inc=1, device_id=dev, device_id_type=MESH)

    @pl.when(off_diag)
    def _():
        hail(at(z, d, y))

    for axis in ("z", "y", "dp"):
        for i in (4, 3, 5, 2, 6, 1, 7):
            hail(along(axis, i))

    S["pad"][...] = jnp.zeros_like(S["pad"])
    S["gown"][...] = jnp.zeros_like(S["gown"])
    for load in small_loads:
        load.wait()
    S["gown"][:, :F] = jnp.broadcast_to(S["go"][...].astype(f32), (8, F))

    @pl.when(off_diag)
    def _():
        pl.semaphore_wait(barrier, 22)

    @pl.when(diag)
    def _():
        pl.semaphore_wait(barrier, 21)

    yield "barrier"
    perm = [
        (S["xo"], S["xg"].at[d, y]),
        (S["to"], S["tg"].at[d, y]),
        (S["gown"], S["gg"].at[y]),
    ]
    perm = [remote(src, dst, "perm", (i,), at(z, d, y)) for i, (src, dst) in enumerate(perm)]

    @pl.when(off_diag)
    def _():
        for copy in perm:
            copy.start()

    @pl.when(diag)
    def _():
        pltpu.make_async_copy(S["xo"], S["xg"].at[z, y], S["perm"].at[1, 0]).start()
        pltpu.make_async_copy(S["to"], S["tg"].at[z, y], S["perm"].at[1, 1]).start()
        pltpu.make_async_copy(S["gown"], S["gg"].at[y], S["perm"].at[1, 2]).start()

    @ends.append
    def _():
        @pl.when(off_diag)
        def _():
            for copy in perm:
                copy.wait_send()

    def first_stage(ref, sem, axis):
        copies = [
            pltpu.make_async_remote_copy(
                src_ref=ref.at[z, y], dst_ref=ref.at[z, y], send_sem=S[sem].at[7], recv_sem=S[sem].at[i - 1],
                device_id=along(axis, i), device_id_type=MESH) for i in range(1, 8)]
        for copy in (copies[i] for i in (3, 2, 4, 1, 5, 0, 6)):
            copy.start()
        ends.append(whole(ref.at[0, pl.ds(0, 7)], S[sem].at[7], S[sem].at[0]).wait_send)
        return copies

    perm[0].wait_recv()
    gx = first_stage(S["xg"], "sx", "z")
    piece = S["xg"][z, y].astype(f32)
    S["sta"][y] = jnp.zeros((8, 128), f32)
    S["sta"][y, 0:1] = jnp.sum(piece, axis=0, keepdims=True)
    S["sta"][y, 1:2] = jnp.sum(piece * piece, axis=0, keepdims=True)
    perm[1].wait_recv()
    gt = first_stage(S["tg"], "stg", "y")
    sta = spread("sta", y, 1, "y")
    perm[2].wait_recv()
    ggain = spread("gg", y, 0, "y")
    yield "permute"

    def offset(e):
        return (e + 1) // 2 if e % 2 else (8 - e // 2) % 8

    def ring_piece(axis, origin, e):
        if isinstance(e, int):
            off = offset(e)
        else:
            off = jnp.where(e % 2 == 1, (e + 1) // 2, (8 - e // 2) % 8)
        if axis == 0:
            return S["xg"].at[(z + off) % 8, origin]
        return S["tg"].at[origin, (y + off) % 8]

    def ring_send(axis, way, k, j, p):
        sign = 1 - 2 * way
        ref = ring_piece(axis, ((y if axis == 0 else z) - sign * (k - 1) + 8) % 8, 2 * j + p)
        pltpu.make_async_remote_copy(
            src_ref=ref, dst_ref=ref, send_sem=S["ring_s"].at[axis, k - 1],
            recv_sem=S["ring_r"].at[axis, way, k - 1, j],
            device_id=along("yz"[axis], sign + 8), device_id_type=MESH).start()

    def ring_wait(axis, way, k, j):
        whole(S["xg"].at[0, pl.ds(0, 2)], S["ring_s"].at[axis, 0], S["ring_r"].at[axis, way, k - 1, j]).wait_recv()

    def ring_rest(k, j, carry):
        for axis in (0, 1):
            for way in (0, 1):
                ring_wait(axis, way, k - 1, j)
                for p in (0, 1):
                    ring_send(axis, way, k, j, p)
        return carry

    def ring_last(j, carry):
        for axis in (0, 1):
            for way in (0, 1):
                ring_wait(axis, way, 3, 2 * j + way)
                for p in (0, 1):
                    ring_send(axis, way, 4, 2 * j + way, p)
        return carry

    for e in range(8):
        for axis in (0, 1):
            if e:
                (gx, gt)[axis][7 - offset(e)].wait_recv()
            for way in (0, 1):
                ring_send(axis, way, 1, e // 2, e % 2)
    for axis in (0, 1):
        for k in (1, 2, 3, 4):
            ends.append(whole(
                S["xg"].at[pl.ds(0, 2)] if k < 4 else S["xg"].at[0],
                S["ring_s"].at[axis, k - 1], S["ring_r"].at[axis, 0, 0, 0]).wait_send)
    yield "ring1"
    arrive(sta)
    S["stb"][d] = jnp.sum(S["sta"][...], axis=0)
    stb = spread("stb", d, 2, "dp")
    lax.fori_loop(0, 4, functools.partial(ring_rest, 2), 0)
    yield "ring2"
    arrive(stb)
    S["stc"][z] = jnp.sum(S["stb"][...], axis=0)
    stc = spread("stc", z, 3, "z")
    lax.fori_loop(0, 4, functools.partial(ring_rest, 3), 0)
    yield "ring3"
    arrive(ggain)
    for load in loads:
        load()
        ends.remove(load)
    total = jnp.zeros((8, H), f32)
    for i in range(8):
        rows = S["gg"][i]
        S["gb"][i] = turned(rows[0:1])[:F]
        total += jnp.dot(rows[:, :F].astype(bf16), S["w1"][F * i:F * (i + 1)], preferred_element_type=f32)
    S["u"][...] = total
    arrive(stc)
    lax.fori_loop(0, 2, ring_last, 0)
    for way in (0, 1):
        ring_wait(0, way, 3, 1 - way)
        ring_wait(0, way, 4, way)
    yield "ringhalf"

    place = [(z + offset(e)) % 8 for e in range(8)]

    def scale_of(tile):
        mean = tile[0:1] / D
        return mean, lax.rsqrt(tile[1:2] / D - mean * mean + epsilon)

    def normed(h):
        for e in range(4 * h, 4 * h + 4):
            mean, inv = scale_of(S["stc"][place[e]])

            def rows(i, carry):
                S["nt"][e, i] = ((S["xg"][place[e], i].astype(f32) - mean) * inv * S["gb"][i]).astype(bf16)
                return carry

            lax.fori_loop(0, 8, rows, 0)

    def joined(ref, spots):
        return jnp.concatenate([ref[i].reshape(K, 128) for i in spots], axis=1)

    def products(h):
        for i in (2 * h, 2 * h + 1):
            lanes = slice(256 * (i % 2), 256 * (i % 2 + 1))
            pre_part = lax.dot_general(
                S["w1"][...], joined(S["nt"], (2 * i, 2 * i + 1)), (((0,), (0,)), ((), ())), preferred_element_type=f32)
            act_part = jnp.dot(S["w2"][...], joined(S["tg"], place[2 * i:2 * i + 2]), preferred_element_type=f32)
            S["part"][h, 0, :, :, :, lanes] = pre_part.reshape(4, 2, Q, 256)
            S["part"][h, 1, :, :, :, lanes] = act_part.reshape(4, 2, Q, 256)
        pairs = {}
        for i in (1, 2, 3, 0):
            to = (chip + i) % 4
            for arr in range(2):
                S["cs"][h, to, arr] = S["part"][h, arr, to, 1 - core].astype(bf16)
            pairs[i] = go(S["cs"].at[h, to], S["cr"].at[h, to], "core", (h, i), at(2 * chip + 1 - core, z, y))
        return pairs

    def chip_sum(h, pairs):
        hops = []
        for i in (1, 2, 3):
            to = (chip + i) % 4
            pairs[i].wait_recv()
            for arr in range(2):
                S["xs"][h, i - 1, arr] = (
                    S["part"][h, arr, to, core] + S["cr"][h, to, arr].astype(f32)).astype(bf16)
            hops.append(go(S["xs"].at[h, i - 1], S["xr"].at[h, i - 1], "xx", (h, i - 1), at(2 * to + core, z, y)))
        return hops

    def activate(h, pairs, hops):
        pairs[0].wait_recv()
        arrive(hops)
        pre_act, act_grad = (
            S["part"][h, arr, chip, core] + S["cr"][h, chip, arr].astype(f32)
            + sum(S["xr"][h, i, arr].astype(f32) for i in range(3)) for arr in range(2))
        value, slope = gelu_parts(pre_act)
        pre_grad = (act_grad * slope).astype(bf16)
        S["comb"][h, d, 0] = value.astype(bf16)
        S["comb"][h, d, 1] = pre_grad
        hops = {
            i: go(S["comb"].at[h, d], S["comb"].at[h, d], "ax", (h, i - 1), at(2 * ((chip + i) % 4) + core, z, y))
            for i in (1, 2, 3)}
        second = jnp.sum(pre_grad.astype(f32) * pre_act, axis=0, keepdims=True)
        for i in range(4):
            S["s2p"][place[4 * h + i]] = jnp.zeros((8, 128), f32)
            S["s2p"][place[4 * h + i], 1:2] = second[:, 128 * i:128 * (i + 1)]
        return hops

    def pass_on(h, hops):
        pairs = []
        for i in (0, 3, 1, 2):
            slot = 2 * ((chip - i + 4) % 4) + core
            if i:
                hops[i].wait_recv()
            ref = S["comb"].at[h, slot]
            pairs.append(go(ref, ref, "ac", (h, i), at(2 * chip + 1 - core, z, y)))
        return pairs

    both = (0, 1)
    normed(0)
    pairs = {0: products(0)}
    hops = {0: chip_sum(0, pairs[0])}
    for way in both:
        ring_wait(0, way, 3, 3 - way)
        ring_wait(0, way, 4, 2 + way)
        for j in both:
            ring_wait(1, way, 3, 2 * j + 1 - way)
            ring_wait(1, way, 4, 2 * j + way)
    normed(1)
    pairs[1] = products(1)
    hops[1] = chip_sum(1, pairs[1])
    yield "chipsum"
    hops = [activate(h, pairs[h], hops[h]) for h in both]
    yield "dpsum"
    pairs = [pass_on(h, hops[h]) for h in both]

    def norm_products(h):
        arrive(pairs[h])
        for i in (2 * h, 2 * h + 1):
            lanes = slice(256 * (i % 2), 256 * (i % 2 + 1))
            out = jnp.dot(
                S["w1"][...], S["comb"][h, :, 1, :, lanes].reshape(H, 256), preferred_element_type=f32)
            S["ng"][2 * i] = out[:, :128].reshape(8, F, 128)
            S["ng"][2 * i + 1] = out[:, 128:].reshape(8, F, 128)

    rs = {}

    def rs_block(axis, dest, h):
        return S["ng"][pl.ds(4 * h, 4), dest, HALF * axis:HALF * (axis + 1)]

    def rs_add(axis, way, k, h, val):
        if (axis, way, k, h) in rs:
            rs[axis, way, k, h].wait_recv()
            val = val + S["ra"][axis, k - 1, way, pl.ds(4 * h, 4)].astype(f32)
        return val

    def rs_round(r, h):
        for axis in both:
            for way in both:
                k = r + 1 if h == way else r + 2
                if k > 4:
                    continue
                sign = 1 - 2 * way
                val = rs_block(axis, (y + sign * (5 - k) + 8) % 8, h)
                val = rs_add(axis, way, k - 1, h, val)
                half = pl.ds(4 * h, 4)
                S["sa"][axis, k - 1, way, half] = val.astype(bf16)
                rs[axis, way, k, h] = pltpu.make_async_remote_copy(
                    src_ref=S["sa"].at[axis, k - 1, way, half], dst_ref=S["ra"].at[axis, k - 1, way, half],
                    send_sem=S["rs_s"].at[axis, k - 1], recv_sem=S["rs_r"].at[axis, way, k - 1, h],
                    device_id=along("y", sign + 8), device_id_type=MESH)
                rs[axis, way, k, h].start()

    yield "passon"
    norm_products(0)
    rs_round(0, 0)
    norm_products(1)
    yield "dpgather"
    rs_round(0, 1)
    def hidden(arr):
        return jnp.concatenate([S["comb"][h, :, arr].reshape(H, 512) for h in both], axis=1)

    pg = hidden(1)
    high = S["u"][...].astype(bf16)
    low = (S["u"][...] - high.astype(f32)).astype(bf16)
    first = jnp.dot(high, pg, preferred_element_type=f32) + jnp.dot(low, pg, preferred_element_type=f32)
    for i in range(8):
        S["s2p"][place[i], 0:1] = first[0:1, 128 * i:128 * (i + 1)]
    s2a = spread("s2r", d, 4, "dp", lambda i: S["s2p"].at[(d + i) % 8])
    S["s2r"][d] = S["s2p"][d]
    rs_round(1, 0)
    rs_round(1, 1)
    arrive(s2a)
    S["s2y"][y] = jnp.sum(S["s2r"][...], axis=0)
    s2b = spread("s2y", y, 5, "y")
    rs_round(2, 0)
    rs_round(2, 1)
    arrive(s2b)
    S["s2z"][z] = jnp.sum(S["s2y"][...], axis=0)
    s2c = spread("s2z", z, 6, "z")
    rs_round(3, 0)
    rs_round(3, 1)
    yield "round3"
    arrive(s2c)
    for axis in both:
        for k in (1, 2, 3, 4):
            ends.append(whole(
                S["sa"].at[axis, k - 1, 0] if k == 1 else S["sa"].at[axis, k - 1],
                S["rs_s"].at[axis, k - 1], S["rs_r"].at[axis, 0, 0, 0]).wait_send)

    def parts(axis):
        for h in both:
            val = rs_block(axis, y, h)
            for way in both:
                val = rs_add(axis, way, 4, h, val)
            for i in range(4):
                S["ng"][4 * h + i, y, HALF * axis:HALF * (axis + 1)] = val[i]
                S["fs"][axis, place[4 * h + i]] = val[i].astype(bf16)
        S["ft"][axis, d] = S["fs"][axis, d]
        return scatter(S["ft"].at[axis], d, 7 + axis, "dp", lambda i: S["fs"].at[axis, (d + i) % 8])

    def to_owners(axis):
        S["fr"][axis, z] = S["ft"][axis, z]
        return scatter(S["fr"].at[axis], z, 9 + axis, "z", lambda i: S["ft"].at[axis, (z + i) % 8])

    blocks = [parts(axis) for axis in both]
    yield "rings"
    total = jnp.zeros((F, 128), f32)
    for i in range(8):
        mean, inv = scale_of(S["stc"][place[i]])
        total += S["ng"][i, y] * ((S["xg"][place[i], y].astype(f32) - mean) * inv)
    S["pad"][:F] = total
    S["gs"][d] = jnp.broadcast_to(jnp.sum(S["pad"][...].T, axis=0, keepdims=True), (8, 128))
    gains = spread("gs", d, 11, "dp")
    arrive(blocks[0])
    owned = [to_owners(0)]
    arrive(blocks[1])
    owned.append(to_owners(1))
    arrive(gains)
    S["gr"][z] = S["gs"][z]
    gain_parts = spread("gr", z, 12, "z", lambda i: S["gs"].at[(z + i) % 8])
    nt_all = joined(S["nt"], range(8))
    S["w1g"][...] = lax.dot_general(nt_all, hidden(1), (((1,), (1,)), ((), ())), preferred_element_type=f32)
    ends.append(local(S["w1g"], w1g_hbm, 5).wait)
    tg_all = joined(S["tg"], place)
    S["w2g"][...] = lax.dot_general(hidden(0), tg_all, (((1,), (1,)), ((), ())), preferred_element_type=f32)
    ends.append(local(S["w2g"], w2g_hbm, 6).wait)
    gcol = turned(S["gown"][0:1])[:F]
    mean, inv = scale_of(S["stc"][d])
    cen = (S["xo"][...].astype(f32) - mean) * inv
    tile = jnp.sum(S["s2z"][...], axis=0)
    base = S["to"][...].astype(f32) - inv * (tile[0:1] / D + cen * (tile[1:2] / D))
    for axis in both:
        arrive(owned[axis])
    grad = jnp.concatenate([jnp.sum(S["fr"][axis].astype(f32), axis=0) for axis in both], axis=0)
    S["igv"][...] = (base + inv * (grad * gcol)).astype(bf16)
    ends.append(local(S["igv"], ig_hbm, 7).wait)
    arrive(gain_parts)
    S["ggv"][...] = jnp.sum(S["gr"][...], axis=0)[0:1, :F]
    ends.append(local(S["ggv"], gg_hbm, 8).wait)


def hand_over(*refs):
    ins, outs, held, sem = refs[:4], refs[4:8], refs[8:12], refs[12]
    steps = []
    for i in (2, 3, 0, 1):
        rows = ins[i].shape[0] // 4
        for part in range(4 if i < 2 else 1):
            span = pl.ds(rows * part, rows) if i < 2 else slice(None)
            steps.append((
                pltpu.make_async_copy(ins[i].at[span], held[i].at[span], sem.at[0, i, part]),
                pltpu.make_async_copy(held[i].at[span], outs[i].at[span], sem.at[1, i, part])))
    for load, _ in steps:
        load.start()
    for load, store in steps:
        load.wait()
        store.start()
    for _, store in steps:
        store.wait()


def shards(inputs, gain, w_in, w_out, targets):
    hbm = pl.BlockSpec(memory_space=pl.ANY)
    scratch = [pltpu.VMEM(shape, kind) for shape, kind in SCRATCH.values()]
    scratch += [pltpu.SemaphoreType.DMA(shape) for shape in SEMS.values()]
    results = (
        jax.ShapeDtypeStruct((K, H), f32), jax.ShapeDtypeStruct((H, K), f32),
        jax.ShapeDtypeStruct((F, 128), bf16), jax.ShapeDtypeStruct((1, F), f32))
    input_grad, gain_grad, w_in_grad, w_out_grad = pl.pallas_call(
        kernel,
        out_shape=(*results[2:], *results[:2]),
        in_specs=[hbm] * 5,
        out_specs=(hbm,) * 4,
        scratch_shapes=scratch,
        compiler_params=pltpu.CompilerParams(
            collective_id=0, has_side_effects=True, vmem_limit_bytes=60 * 1024 * 1024),
        cost_estimate=pl.CostEstimate(flops=2 * 10 ** 9, bytes_accessed=4 * 10 ** 6, transcendentals=10 ** 5),
        name="backward",
    )(inputs.T, targets.T, gain.reshape(1, F), w_in, w_out)
    w_in_grad, w_out_grad, input_grad, gain_grad = pl.pallas_call(
        hand_over,
        out_shape=results,
        in_specs=[hbm] * 4,
        out_specs=(hbm,) * 4,
        scratch_shapes=[pltpu.VMEM(out.shape, out.dtype) for out in results] + [pltpu.SemaphoreType.DMA((2, 4, 4))],
        compiler_params=pltpu.CompilerParams(vmem_limit_bytes=60 * 1024 * 1024),
        cost_estimate=pl.CostEstimate(flops=0, bytes_accessed=3 * 10 ** 6, transcendentals=0),
        name="hand_over",
    )(w_in_grad, w_out_grad, input_grad, gain_grad)
    return input_grad.T, gain_grad.reshape(F), w_in_grad, w_out_grad


def solution(mesh):
    return jax.shard_map(
        shards,
        mesh=mesh,
        in_specs=(P("dp", "mp"), P("mp"), P("dp", "mp"), P("mp", "dp"), P("dp", "mp")),
        out_specs=(P("dp", "mp"), P("mp"), P("dp", "mp"), P("mp", "dp")),
        check_vma=False,
    )
```

```python
import functools

import jax
import jax.numpy as jnp
from jax import lax
from jax.experimental import pallas as pl
from jax.experimental.pallas import tpu as pltpu
from jax.sharding import PartitionSpec as P

epsilon = 1e-06
MESH = pl.DeviceIdType.MESH
bf16, f32 = jnp.bfloat16, jnp.float32
D = 6144
F = 96
K = 768
H = 256
Q = 32
HALF = F // 2


def gelu_parts(values):
    cumul = 0.5 * (1.0 + lax.erf(values * 0.7071067811865476))
    slope = cumul + values * jnp.exp(-0.5 * values * values) * 0.3989422804014327
    return values * cumul, slope


def turned(rows):
    return jnp.broadcast_to(rows, (128, 128)).T


SCRATCH = dict(
    w1=((K, H), bf16), w2=((H, K), bf16),
    pad=((128, 128), f32), xo=((F, 128), bf16), to=((F, 128), bf16), go=((1, F), bf16),
    igv=((F, 128), bf16), ggv=((1, F), f32), gown=((8, 128), f32),
    xg=((8, 8, F, 128), bf16), tg=((8, 8, F, 128), bf16), nt=((8, 8, F, 128), bf16),
    gg=((8, 8, 128), f32), gb=((8, F, 128), f32),
    sta=((8, 8, 128), f32), stb=((8, 8, 128), f32), stc=((8, 8, 128), f32),
    part=((2, 2, 4, 2, Q, 512), f32), cs=((2, 4, 2, Q, 512), bf16), cr=((2, 4, 2, Q, 512), bf16),
    xs=((2, 3, 2, Q, 512), bf16), xr=((2, 3, 2, Q, 512), bf16), comb=((2, 8, 2, Q, 512), bf16),
    u=((8, H), f32), s2p=((8, 8, 128), f32), s2r=((8, 8, 128), f32),
    s2y=((8, 8, 128), f32), s2z=((8, 8, 128), f32),
    ng=((8, 8, F, 128), f32), ra=((2, 4, 2, 8, HALF, 128), bf16), sa=((2, 4, 2, 8, HALF, 128), bf16),
    fs=((2, 8, HALF, 128), bf16), ft=((2, 8, HALF, 128), bf16), fr=((2, 8, HALF, 128), bf16),
    w1g=((K, H), f32), w2g=((H, K), f32), gs=((8, 8, 128), f32), gr=((8, 8, 128), f32),
)
SEMS = dict(
    loc=(9,), perm=(2, 3), sx=(8,), stg=(8,), small=(2, 13), ring_s=(2, 4), ring_r=(2, 2, 4, 4),
    core=(2, 2, 4), xx=(2, 2, 3), ax=(2, 2, 3), ac=(2, 2, 4), rs_s=(2, 4), rs_r=(2, 2, 4, 2),
)


def kernel(*refs):
    ends = []
    for _ in phases(ends, *refs):
        pass
    for end in ends:
        end()


def phases(ends, x_hbm, t_hbm, g_hbm, w1_hbm, w2_hbm, ig_hbm, gg_hbm, w1g_hbm, w2g_hbm, *scratch):
    S = dict(zip(list(SCRATCH) + list(SEMS), scratch, strict=True))
    d, m = lax.axis_index("dp"), lax.axis_index("mp")
    z, y = m // 8, m % 8
    chip, core = d // 2, d % 2
    diag = d == z
    off_diag = jnp.logical_not(diag)

    def at(dp, zz, yy):
        return (dp, zz * 8 + yy)

    def remote(src, dst, sem, index, dev):
        return pltpu.make_async_remote_copy(
            src_ref=src, dst_ref=dst, send_sem=S[sem].at[(0, *index)],
            recv_sem=S[sem].at[(1, *index)], device_id=dev, device_id_type=MESH)

    def whole(ref, send_sem, recv_sem):
        return pltpu.make_async_remote_copy(
            src_ref=ref, dst_ref=ref, send_sem=send_sem, recv_sem=recv_sem,
            device_id=at(z, d, y), device_id_type=MESH)

    def go(src, dst, sem, index, dev):
        copy = remote(src, dst, sem, index, dev)
        copy.start()
        ends.append(copy.wait_send)
        return copy

    def along(axis, i):
        if axis == "dp":
            return at((d + i) % 8, z, y)
        if axis == "z":
            return at(d, (z + i) % 8, y)
        return at(d, z, (y + i) % 8)

    def scatter(ref, slot, number, axis, source=None):
        for i in range(1, 8):
            src = ref.at[slot] if source is None else source(i)
            remote(src, ref.at[slot], "small", (number,), along(axis, i)).start()
        seven = whole(ref.at[pl.ds(0, 7)], S["small"].at[0, number], S["small"].at[1, number])
        ends.append(seven.wait_send)
        return [seven]

    def spread(buf, *rest):
        return scatter(S[buf], *rest)

    def arrive(copies):
        for copy in copies:
            copy.wait_recv()

    def local(src, dst, number):
        copy = pltpu.make_async_copy(src, dst, S["loc"].at[number])
        copy.start()
        return copy

    small_loads = [local(ref, S[name], i) for i, (ref, name) in enumerate(((x_hbm, "xo"), (t_hbm, "to"), (g_hbm, "go")))]
    loads = [local(w1_hbm, S["w1"], 3).wait, local(w2_hbm, S["w2"], 4).wait]
    ends.extend(loads)

    barrier = pltpu.get_barrier_semaphore()

    def hail(dev):
        pl.semaphore_signal(barrier, inc=1, device_id=dev, device_id_type=MESH)

    @pl.when(off_diag)
    def _():
        hail(at(z, d, y))

    for axis in ("z", "y", "dp"):
        for i in (4, 3, 5, 2, 6, 1, 7):
            hail(along(axis, i))

    S["pad"][...] = jnp.zeros_like(S["pad"])
    S["gown"][...] = jnp.zeros_like(S["gown"])
    for load in small_loads:
        load.wait()
    S["gown"][:, :F] = jnp.broadcast_to(S["go"][...].astype(f32), (8, F))

    @pl.when(off_diag)
    def _():
        pl.semaphore_wait(barrier, 22)

    @pl.when(diag)
    def _():
        pl.semaphore_wait(barrier, 21)

    yield "barrier"
    perm = [
        (S["xo"], S["xg"].at[d, y]),
        (S["to"], S["tg"].at[d, y]),
        (S["gown"], S["gg"].at[y]),
    ]
    perm = [remote(src, dst, "perm", (i,), at(z, d, y)) for i, (src, dst) in enumerate(perm)]

    @pl.when(off_diag)
    def _():
        for copy in perm:
            copy.start()

    @pl.when(diag)
    def _():
        pltpu.make_async_copy(S["xo"], S["xg"].at[z, y], S["perm"].at[1, 0]).start()
        pltpu.make_async_copy(S["to"], S["tg"].at[z, y], S["perm"].at[1, 1]).start()
        pltpu.make_async_copy(S["gown"], S["gg"].at[y], S["perm"].at[1, 2]).start()

    @ends.append
    def _():
        @pl.when(off_diag)
        def _():
            for copy in perm:
                copy.wait_send()

    def first_stage(ref, sem, axis):
        copies = [
            pltpu.make_async_remote_copy(
                src_ref=ref.at[z, y], dst_ref=ref.at[z, y], send_sem=S[sem].at[7], recv_sem=S[sem].at[i - 1],
                device_id=along(axis, i), device_id_type=MESH) for i in range(1, 8)]
        for copy in (copies[i] for i in (0, 6, 1, 5, 2, 4, 3)):
            copy.start()
        ends.append(whole(ref.at[0, pl.ds(0, 7)], S[sem].at[7], S[sem].at[0]).wait_send)
        return copies

    perm[0].wait_recv()
    gx = first_stage(S["xg"], "sx", "z")
    perm[1].wait_recv()
    gt = first_stage(S["tg"], "stg", "y")
    piece = S["xg"][z, y].astype(f32)
    S["sta"][y] = jnp.zeros((8, 128), f32)
    S["sta"][y, 0:1] = jnp.sum(piece, axis=0, keepdims=True)
    S["sta"][y, 1:2] = jnp.sum(piece * piece, axis=0, keepdims=True)
    sta = spread("sta", y, 1, "y")
    perm[2].wait_recv()
    ggain = spread("gg", y, 0, "y")
    yield "permute"

    def offset(e):
        return (e + 1) // 2 if e % 2 else (8 - e // 2) % 8

    def ring_piece(axis, origin, e):
        if isinstance(e, int):
            off = offset(e)
        else:
            off = jnp.where(e % 2 == 1, (e + 1) // 2, (8 - e // 2) % 8)
        if axis == 0:
            return S["xg"].at[(z + off) % 8, origin]
        return S["tg"].at[origin, (y + off) % 8]

    def ring_send(axis, way, k, j, p):
        sign = 1 - 2 * way
        ref = ring_piece(axis, ((y if axis == 0 else z) - sign * (k - 1) + 8) % 8, 2 * j + p)
        pltpu.make_async_remote_copy(
            src_ref=ref, dst_ref=ref, send_sem=S["ring_s"].at[axis, k - 1],
            recv_sem=S["ring_r"].at[axis, way, k - 1, j],
            device_id=along("yz"[axis], sign + 8), device_id_type=MESH).start()

    def ring_wait(axis, way, k, j):
        whole(S["xg"].at[0, pl.ds(0, 2)], S["ring_s"].at[axis, 0], S["ring_r"].at[axis, way, k - 1, j]).wait_recv()

    def ring_rest(k, j, carry):
        for axis in (0, 1):
            for way in (0, 1):
                ring_wait(axis, way, k - 1, j)
                for p in (0, 1):
                    ring_send(axis, way, k, j, p)
        return carry

    def ring_last(j, carry):
        for axis in (0, 1):
            for way in (0, 1):
                ring_wait(axis, way, 3, 2 * j + way)
                for p in (0, 1):
                    ring_send(axis, way, 4, 2 * j + way, p)
        return carry

    for e in range(8):
        if e == 6:
            arrive(sta)
            S["stb"][d] = jnp.sum(S["sta"][...], axis=0)
            stb = spread("stb", d, 2, "dp")
        for axis in (0, 1):
            if e:
                (gx, gt)[axis][7 - offset(e)].wait_recv()
            for way in (0, 1):
                ring_send(axis, way, 1, e // 2, e % 2)
    for axis in (0, 1):
        for k in (1, 2, 3, 4):
            ends.append(whole(
                S["xg"].at[pl.ds(0, 2)] if k < 4 else S["xg"].at[0],
                S["ring_s"].at[axis, k - 1], S["ring_r"].at[axis, 0, 0, 0]).wait_send)
    lax.fori_loop(0, 4, functools.partial(ring_rest, 2), 0)
    yield "ring2"
    arrive(stb)
    S["stc"][z] = jnp.sum(S["stb"][...], axis=0)
    stc = spread("stc", z, 3, "z")
    lax.fori_loop(0, 4, functools.partial(ring_rest, 3), 0)
    lax.fori_loop(0, 2, ring_last, 0)
    arrive(ggain)
    for load in loads:
        load()
        ends.remove(load)
    total = jnp.zeros((8, H), f32)
    for i in range(8):
        rows = S["gg"][i]
        S["gb"][i] = turned(rows[0:1])[:F]
        total += jnp.dot(rows[:, :F].astype(bf16), S["w1"][F * i:F * (i + 1)], preferred_element_type=f32)
    S["u"][...] = total
    arrive(stc)
    for way in (0, 1):
        ring_wait(0, way, 3, 1 - way)
        ring_wait(0, way, 4, way)
    yield "ringhalf"

    place = [(z + offset(e)) % 8 for e in range(8)]

    def scale_of(tile):
        mean = tile[0:1] / D
        return mean, lax.rsqrt(tile[1:2] / D - mean * mean + epsilon)

    def normed(h):
        for e in range(4 * h, 4 * h + 4):
            mean, inv = scale_of(S["stc"][place[e]])

            def rows(i, carry):
                S["nt"][e, i] = ((S["xg"][place[e], i].astype(f32) - mean) * inv * S["gb"][i]).astype(bf16)
                return carry

            lax.fori_loop(0, 8, rows, 0)

    def joined(ref, spots):
        return jnp.concatenate([ref[i].reshape(K, 128) for i in spots], axis=1)

    def products(h):
        for i in (2 * h, 2 * h + 1):
            lanes = slice(256 * (i % 2), 256 * (i % 2 + 1))
            pre_part = lax.dot_general(
                S["w1"][...], joined(S["nt"], (2 * i, 2 * i + 1)), (((0,), (0,)), ((), ())), preferred_element_type=f32)
            act_part = jnp.dot(S["w2"][...], joined(S["tg"], place[2 * i:2 * i + 2]), preferred_element_type=f32)
            S["part"][h, 0, :, :, :, lanes] = pre_part.reshape(4, 2, Q, 256)
            S["part"][h, 1, :, :, :, lanes] = act_part.reshape(4, 2, Q, 256)
        pairs = {}
        for i in (1, 2, 3, 0):
            to = (chip + i) % 4
            for arr in range(2):
                S["cs"][h, to, arr] = S["part"][h, arr, to, 1 - core].astype(bf16)
            pairs[i] = go(S["cs"].at[h, to], S["cr"].at[h, to], "core", (h, i), at(2 * chip + 1 - core, z, y))
        return pairs

    def chip_sum(h, pairs):
        hops = []
        for i in (1, 2, 3):
            to = (chip + i) % 4
            pairs[i].wait_recv()
            for arr in range(2):
                S["xs"][h, i - 1, arr] = (
                    S["part"][h, arr, to, core] + S["cr"][h, to, arr].astype(f32)).astype(bf16)
            hops.append(go(S["xs"].at[h, i - 1], S["xr"].at[h, i - 1], "xx", (h, i - 1), at(2 * to + core, z, y)))
        return hops

    def activate(h, pairs, hops):
        pairs[0].wait_recv()
        arrive(hops)
        pre_act, act_grad = (
            S["part"][h, arr, chip, core] + S["cr"][h, chip, arr].astype(f32)
            + sum(S["xr"][h, i, arr].astype(f32) for i in range(3)) for arr in range(2))
        value, slope = gelu_parts(pre_act)
        pre_grad = (act_grad * slope).astype(bf16)
        S["comb"][h, d, 0] = value.astype(bf16)
        S["comb"][h, d, 1] = pre_grad
        hops = {
            i: go(S["comb"].at[h, d], S["comb"].at[h, d], "ax", (h, i - 1), at(2 * ((chip + i) % 4) + core, z, y))
            for i in (1, 2, 3)}
        second = jnp.sum(pre_grad.astype(f32) * pre_act, axis=0, keepdims=True)
        for i in range(4):
            S["s2p"][place[4 * h + i]] = jnp.zeros((8, 128), f32)
            S["s2p"][place[4 * h + i], 1:2] = second[:, 128 * i:128 * (i + 1)]
        return hops

    def pass_on(h, hops):
        pairs = []
        for i in (0, 3, 1, 2):
            slot = 2 * ((chip - i + 4) % 4) + core
            if i:
                hops[i].wait_recv()
            ref = S["comb"].at[h, slot]
            pairs.append(go(ref, ref, "ac", (h, i), at(2 * chip + 1 - core, z, y)))
        return pairs

    both = (0, 1)
    normed(0)
    pairs = {0: products(0)}
    hops = {0: chip_sum(0, pairs[0])}
    for way in both:
        ring_wait(0, way, 3, 3 - way)
        ring_wait(0, way, 4, 2 + way)
        for j in both:
            ring_wait(1, way, 3, 2 * j + 1 - way)
            ring_wait(1, way, 4, 2 * j + way)
    normed(1)
    pairs[1] = products(1)
    hops[1] = chip_sum(1, pairs[1])
    yield "chipsum"
    hops = [activate(h, pairs[h], hops[h]) for h in both]
    yield "dpsum"
    pairs = [pass_on(h, hops[h]) for h in both]

    def norm_products(h):
        arrive(pairs[h])
        for i in (2 * h, 2 * h + 1):
            lanes = slice(256 * (i % 2), 256 * (i % 2 + 1))
            out = jnp.dot(
                S["w1"][...], S["comb"][h, :, 1, :, lanes].reshape(H, 256), preferred_element_type=f32)
            S["ng"][2 * i] = out[:, :128].reshape(8, F, 128)
            S["ng"][2 * i + 1] = out[:, 128:].reshape(8, F, 128)

    rs = {}

    def rs_block(axis, dest, h):
        return S["ng"][pl.ds(4 * h, 4), dest, HALF * axis:HALF * (axis + 1)]

    def rs_add(axis, way, k, h, val):
        if (axis, way, k, h) in rs:
            rs[axis, way, k, h].wait_recv()
            val = val + S["ra"][axis, k - 1, way, pl.ds(4 * h, 4)].astype(f32)
        return val

    def rs_round(r, h):
        for axis in both:
            for way in both:
                k = r + 1 if h == way else r + 2
                if k > 4:
                    continue
                sign = 1 - 2 * way
                val = rs_block(axis, (y + sign * (5 - k) + 8) % 8, h)
                val = rs_add(axis, way, k - 1, h, val)
                half = pl.ds(4 * h, 4)
                S["sa"][axis, k - 1, way, half] = val.astype(bf16)
                rs[axis, way, k, h] = pltpu.make_async_remote_copy(
                    src_ref=S["sa"].at[axis, k - 1, way, half], dst_ref=S["ra"].at[axis, k - 1, way, half],
                    send_sem=S["rs_s"].at[axis, k - 1], recv_sem=S["rs_r"].at[axis, way, k - 1, h],
                    device_id=along("y", sign + 8), device_id_type=MESH)
                rs[axis, way, k, h].start()

    yield "passon"
    norm_products(0)
    rs_round(0, 0)
    norm_products(1)
    yield "dpgather"
    rs_round(0, 1)
    def hidden(arr):
        return jnp.concatenate([S["comb"][h, :, arr].reshape(H, 512) for h in both], axis=1)

    pg = hidden(1)
    high = S["u"][...].astype(bf16)
    low = (S["u"][...] - high.astype(f32)).astype(bf16)
    first = jnp.dot(high, pg, preferred_element_type=f32) + jnp.dot(low, pg, preferred_element_type=f32)
    for i in range(8):
        S["s2p"][place[i], 0:1] = first[0:1, 128 * i:128 * (i + 1)]
    s2a = spread("s2r", d, 4, "dp", lambda i: S["s2p"].at[(d + i) % 8])
    S["s2r"][d] = S["s2p"][d]
    rs_round(1, 0)
    rs_round(1, 1)
    arrive(s2a)
    S["s2y"][y] = jnp.sum(S["s2r"][...], axis=0)
    rs_round(2, 0)
    rs_round(2, 1)
    s2b = spread("s2y", y, 5, "y")
    rs_round(3, 0)
    rs_round(3, 1)
    for axis in both:
        for k in (1, 2, 3, 4):
            ends.append(whole(
                S["sa"].at[axis, k - 1, 0] if k == 1 else S["sa"].at[axis, k - 1],
                S["rs_s"].at[axis, k - 1], S["rs_r"].at[axis, 0, 0, 0]).wait_send)

    def parts(axis):
        for h in both:
            val = rs_block(axis, y, h)
            for way in both:
                val = rs_add(axis, way, 4, h, val)
            for i in range(4):
                S["ng"][4 * h + i, y, HALF * axis:HALF * (axis + 1)] = val[i]
                S["fs"][axis, place[4 * h + i]] = val[i].astype(bf16)
        S["ft"][axis, d] = S["fs"][axis, d]
        return scatter(S["ft"].at[axis], d, 7 + axis, "dp", lambda i: S["fs"].at[axis, (d + i) % 8])

    def to_owners(axis):
        S["fr"][axis, z] = S["ft"][axis, z]
        return scatter(S["fr"].at[axis], z, 9 + axis, "z", lambda i: S["ft"].at[axis, (z + i) % 8])

    blocks = [parts(axis) for axis in both]
    yield "rings"
    total = jnp.zeros((F, 128), f32)
    for i in range(8):
        mean, inv = scale_of(S["stc"][place[i]])
        total += S["ng"][i, y] * ((S["xg"][place[i], y].astype(f32) - mean) * inv)
    S["pad"][:F] = total
    S["gs"][d] = jnp.broadcast_to(jnp.sum(S["pad"][...].T, axis=0, keepdims=True), (8, 128))
    gains = spread("gs", d, 11, "dp")
    arrive(s2b)
    S["s2z"][z] = jnp.sum(S["s2y"][...], axis=0)
    arrive(blocks[0])
    owned = [to_owners(0)]
    arrive(blocks[1])
    owned.append(to_owners(1))
    arrive(gains)
    S["gr"][z] = S["gs"][z]
    gain_parts = spread("gr", z, 12, "z", lambda i: S["gs"].at[(z + i) % 8])
    s2c = spread("s2z", z, 6, "z")
    nt_all = joined(S["nt"], range(8))
    S["w1g"][...] = lax.dot_general(nt_all, hidden(1), (((1,), (1,)), ((), ())), preferred_element_type=f32)
    ends.append(local(S["w1g"], w1g_hbm, 5).wait)
    tg_all = joined(S["tg"], place)
    S["w2g"][...] = lax.dot_general(hidden(0), tg_all, (((1,), (1,)), ((), ())), preferred_element_type=f32)
    ends.append(local(S["w2g"], w2g_hbm, 6).wait)
    gcol = turned(S["gown"][0:1])[:F]
    mean, inv = scale_of(S["stc"][d])
    cen = (S["xo"][...].astype(f32) - mean) * inv
    arrive(s2c)
    tile = jnp.sum(S["s2z"][...], axis=0)
    base = S["to"][...].astype(f32) - inv * (tile[0:1] / D + cen * (tile[1:2] / D))
    for axis in both:
        arrive(owned[axis])
    grad = jnp.concatenate([jnp.sum(S["fr"][axis].astype(f32), axis=0) for axis in both], axis=0)
    S["igv"][...] = (base + inv * (grad * gcol)).astype(bf16)
    ends.append(local(S["igv"], ig_hbm, 7).wait)
    arrive(gain_parts)
    S["ggv"][...] = jnp.sum(S["gr"][...], axis=0)[0:1, :F]
    ends.append(local(S["ggv"], gg_hbm, 8).wait)


def hand_over(*refs):
    ins, outs, held, sem = refs[:4], refs[4:8], refs[8:12], refs[12]
    steps = []
    for i in (2, 3, 0, 1):
        rows = ins[i].shape[0] // 4
        for part in range(4 if i < 2 else 1):
            span = pl.ds(rows * part, rows) if i < 2 else slice(None)
            steps.append((
                pltpu.make_async_copy(ins[i].at[span], held[i].at[span], sem.at[0, i, part]),
                pltpu.make_async_copy(held[i].at[span], outs[i].at[span], sem.at[1, i, part])))
    for load, _ in steps:
        load.start()
    for load, store in steps:
        load.wait()
        store.start()
    for _, store in steps:
        store.wait()


def shards(inputs, gain, w_in, w_out, targets):
    hbm = pl.BlockSpec(memory_space=pl.ANY)
    scratch = [pltpu.VMEM(shape, kind) for shape, kind in SCRATCH.values()]
    scratch += [pltpu.SemaphoreType.DMA(shape) for shape in SEMS.values()]
    results = (
        jax.ShapeDtypeStruct((K, H), f32), jax.ShapeDtypeStruct((H, K), f32),
        jax.ShapeDtypeStruct((F, 128), bf16), jax.ShapeDtypeStruct((1, F), f32))
    input_grad, gain_grad, w_in_grad, w_out_grad = pl.pallas_call(
        kernel,
        out_shape=(*results[2:], *results[:2]),
        in_specs=[hbm] * 5,
        out_specs=(hbm,) * 4,
        scratch_shapes=scratch,
        compiler_params=pltpu.CompilerParams(
            collective_id=0, has_side_effects=True, vmem_limit_bytes=60 * 1024 * 1024),
        cost_estimate=pl.CostEstimate(flops=2 * 10 ** 9, bytes_accessed=4 * 10 ** 6, transcendentals=10 ** 5),
        name="backward",
    )(inputs.T, targets.T, gain.reshape(1, F), w_in, w_out)
    w_in_grad, w_out_grad, input_grad, gain_grad = pl.pallas_call(
        hand_over,
        out_shape=results,
        in_specs=[hbm] * 4,
        out_specs=(hbm,) * 4,
        scratch_shapes=[pltpu.VMEM(out.shape, out.dtype) for out in results] + [pltpu.SemaphoreType.DMA((2, 4, 4))],
        compiler_params=pltpu.CompilerParams(vmem_limit_bytes=60 * 1024 * 1024),
        cost_estimate=pl.CostEstimate(flops=0, bytes_accessed=3 * 10 ** 6, transcendentals=0),
        name="hand_over",
    )(w_in_grad, w_out_grad, input_grad, gain_grad)
    return input_grad.T, gain_grad.reshape(F), w_in_grad, w_out_grad


def solution(mesh):
    return jax.shard_map(
        shards,
        mesh=mesh,
        in_specs=(P("dp", "mp"), P("mp"), P("dp", "mp"), P("mp", "dp"), P("dp", "mp")),
        out_specs=(P("dp", "mp"), P("mp"), P("dp", "mp"), P("mp", "dp")),
        check_vma=False,
    )
```

```python
import functools

import jax
import jax.numpy as jnp
from jax import lax
from jax.experimental import pallas as pl
from jax.experimental.pallas import tpu as pltpu
from jax.sharding import PartitionSpec as P

epsilon = 1e-06
MESH = pl.DeviceIdType.MESH
bf16, f32 = jnp.bfloat16, jnp.float32
D = 6144
F = 96
K = 768
H = 256
Q = 32
HALF = F // 2


def gelu_parts(values):
    cumul = 0.5 * (1.0 + lax.erf(values * 0.7071067811865476))
    slope = cumul + values * jnp.exp(-0.5 * values * values) * 0.3989422804014327
    return values * cumul, slope


def turned(rows):
    return jnp.broadcast_to(rows, (128, 128)).T


SCRATCH = dict(
    w1=((K, H), bf16), w2=((H, K), bf16),
    pad=((128, 128), f32), xo=((F, 128), bf16), to=((F, 128), bf16), go=((1, F), bf16),
    igv=((F, 128), bf16), ggv=((1, F), f32), gown=((8, 128), f32),
    xg=((8, 8, F, 128), bf16), tg=((8, 8, F, 128), bf16), nt=((8, 8, F, 128), bf16),
    gg=((8, 8, 128), f32), gb=((8, F, 128), f32),
    sta=((8, 8, 128), f32), stb=((8, 8, 128), f32), stc=((8, 8, 128), f32),
    part=((2, 2, 4, 2, Q, 512), f32), cs=((2, 4, 2, Q, 512), bf16), cr=((2, 4, 2, Q, 512), bf16),
    xs=((2, 3, 2, Q, 512), bf16), xr=((2, 3, 2, Q, 512), bf16), comb=((2, 8, 2, Q, 512), bf16),
    u=((8, H), f32), s2p=((8, 8, 128), f32), s2r=((8, 8, 128), f32),
    s2y=((8, 8, 128), f32), s2z=((8, 8, 128), f32),
    ng=((8, 8, F, 128), f32), ra=((2, 4, 2, 8, HALF, 128), bf16), sa=((2, 4, 2, 8, HALF, 128), bf16),
    fs=((2, 8, HALF, 128), bf16), ft=((2, 8, HALF, 128), bf16), fr=((2, 8, HALF, 128), bf16),
    w1g=((K, H), f32), w2g=((H, K), f32), gs=((8, 8, 128), f32), gr=((8, 8, 128), f32),
)
SEMS = dict(
    loc=(9,), perm=(2, 3), sx=(8,), stg=(8,), small=(2, 13), ring_s=(2, 4), ring_r=(2, 2, 4, 4),
    core=(2, 2, 4), xx=(2, 2, 3), ax=(2, 2, 3), ac=(2, 2, 4), rs_s=(2, 4), rs_r=(2, 2, 4, 2),
)


def kernel(*refs):
    ends = []
    for _ in phases(ends, *refs):
        pass
    for end in ends:
        end()


def phases(ends, x_hbm, t_hbm, g_hbm, w1_hbm, w2_hbm, ig_hbm, gg_hbm, w1g_hbm, w2g_hbm, *scratch):
    S = dict(zip(list(SCRATCH) + list(SEMS), scratch, strict=True))
    d, m = lax.axis_index("dp"), lax.axis_index("mp")
    z, y = m // 8, m % 8
    chip, core = d // 2, d % 2
    diag = d == z
    off_diag = jnp.logical_not(diag)

    def at(dp, zz, yy):
        return (dp, zz * 8 + yy)

    def remote(src, dst, sem, index, dev):
        return pltpu.make_async_remote_copy(
            src_ref=src, dst_ref=dst, send_sem=S[sem].at[(0, *index)],
            recv_sem=S[sem].at[(1, *index)], device_id=dev, device_id_type=MESH)

    def whole(ref, send_sem, recv_sem):
        return pltpu.make_async_remote_copy(
            src_ref=ref, dst_ref=ref, send_sem=send_sem, recv_sem=recv_sem,
            device_id=at(z, d, y), device_id_type=MESH)

    def go(src, dst, sem, index, dev):
        copy = remote(src, dst, sem, index, dev)
        copy.start()
        ends.append(copy.wait_send)
        return copy

    def along(axis, i):
        if axis == "dp":
            return at((d + i) % 8, z, y)
        if axis == "z":
            return at(d, (z + i) % 8, y)
        return at(d, z, (y + i) % 8)

    def scatter(ref, slot, number, axis, source=None):
        for i in range(1, 8):
            src = ref.at[slot] if source is None else source(i)
            remote(src, ref.at[slot], "small", (number,), along(axis, i)).start()
        seven = whole(ref.at[pl.ds(0, 7)], S["small"].at[0, number], S["small"].at[1, number])
        ends.append(seven.wait_send)
        return [seven]

    def spread(buf, *rest):
        return scatter(S[buf], *rest)

    def arrive(copies):
        for copy in copies:
            copy.wait_recv()

    def local(src, dst, number):
        copy = pltpu.make_async_copy(src, dst, S["loc"].at[number])
        copy.start()
        return copy

    small_loads = [local(ref, S[name], i) for i, (ref, name) in enumerate(((x_hbm, "xo"), (t_hbm, "to"), (g_hbm, "go")))]
    loads = [local(w1_hbm, S["w1"], 3).wait, local(w2_hbm, S["w2"], 4).wait]
    ends.extend(loads)

    barrier = pltpu.get_barrier_semaphore()

    def hail(dev):
        pl.semaphore_signal(barrier, inc=1, device_id=dev, device_id_type=MESH)

    @pl.when(off_diag)
    def _():
        hail(at(z, d, y))

    for axis in ("z", "y", "dp"):
        for i in (4, 3, 5, 2, 6, 1, 7):
            hail(along(axis, i))

    S["pad"][...] = jnp.zeros_like(S["pad"])
    S["gown"][...] = jnp.zeros_like(S["gown"])
    for load in small_loads:
        load.wait()
    S["gown"][:, :F] = jnp.broadcast_to(S["go"][...].astype(f32), (8, F))

    @pl.when(off_diag)
    def _():
        pl.semaphore_wait(barrier, 22)

    @pl.when(diag)
    def _():
        pl.semaphore_wait(barrier, 21)

    yield "barrier"
    perm = [
        (S["xo"], S["xg"].at[d, y]),
        (S["to"], S["tg"].at[d, y]),
        (S["gown"], S["gg"].at[y]),
    ]
    perm = [remote(src, dst, "perm", (i,), at(z, d, y)) for i, (src, dst) in enumerate(perm)]

    @pl.when(off_diag)
    def _():
        for copy in perm:
            copy.start()

    @pl.when(diag)
    def _():
        pltpu.make_async_copy(S["xo"], S["xg"].at[z, y], S["perm"].at[1, 0]).start()
        pltpu.make_async_copy(S["to"], S["tg"].at[z, y], S["perm"].at[1, 1]).start()
        pltpu.make_async_copy(S["gown"], S["gg"].at[y], S["perm"].at[1, 2]).start()

    @ends.append
    def _():
        @pl.when(off_diag)
        def _():
            for copy in perm:
                copy.wait_send()

    def first_stage(ref, sem, axis):
        copies = [
            pltpu.make_async_remote_copy(
                src_ref=ref.at[z, y], dst_ref=ref.at[z, y], send_sem=S[sem].at[7], recv_sem=S[sem].at[i - 1],
                device_id=along(axis, i), device_id_type=MESH) for i in range(1, 8)]
        for copy in (copies[i] for i in (0, 6, 1, 5, 2, 4, 3)):
            copy.start()
        ends.append(whole(ref.at[0, pl.ds(0, 7)], S[sem].at[7], S[sem].at[0]).wait_send)
        return copies

    perm[0].wait_recv()
    gx = first_stage(S["xg"], "sx", "z")
    perm[1].wait_recv()
    gt = first_stage(S["tg"], "stg", "y")
    piece = S["xg"][z, y].astype(f32)
    S["sta"][y] = jnp.zeros((8, 128), f32)
    S["sta"][y, 0:1] = jnp.sum(piece, axis=0, keepdims=True)
    S["sta"][y, 1:2] = jnp.sum(piece * piece, axis=0, keepdims=True)
    sta = spread("sta", y, 1, "y")
    perm[2].wait_recv()
    ggain = spread("gg", y, 0, "y")
    yield "permute"

    def offset(e):
        return (e + 1) // 2 if e % 2 else (8 - e // 2) % 8

    def ring_piece(axis, origin, e):
        if isinstance(e, int):
            off = offset(e)
        else:
            off = jnp.where(e % 2 == 1, (e + 1) // 2, (8 - e // 2) % 8)
        if axis == 0:
            return S["xg"].at[(z + off) % 8, origin]
        return S["tg"].at[origin, (y + off) % 8]

    def ring_send(axis, way, k, j, p):
        sign = 1 - 2 * way
        ref = ring_piece(axis, ((y if axis == 0 else z) - sign * (k - 1) + 8) % 8, 2 * j + p)
        pltpu.make_async_remote_copy(
            src_ref=ref, dst_ref=ref, send_sem=S["ring_s"].at[axis, k - 1],
            recv_sem=S["ring_r"].at[axis, way, k - 1, j],
            device_id=along("yz"[axis], sign + 8), device_id_type=MESH).start()

    def ring_wait(axis, way, k, j):
        whole(S["xg"].at[0, pl.ds(0, 2)], S["ring_s"].at[axis, 0], S["ring_r"].at[axis, way, k - 1, j]).wait_recv()

    def ring_rest(k, j, carry):
        for axis in (0, 1):
            for way in (0, 1):
                ring_wait(axis, way, k - 1, j)
                for p in (0, 1):
                    ring_send(axis, way, k, j, p)
        return carry

    def ring_last(j, carry):
        for axis in (0, 1):
            for way in (0, 1):
                ring_wait(axis, way, 3, 2 * j + way)
                for p in (0, 1):
                    ring_send(axis, way, 4, 2 * j + way, p)
        return carry

    for e in range(8):
        if e == 6:
            arrive(sta)
            S["stb"][d] = jnp.sum(S["sta"][...], axis=0)
            stb = spread("stb", d, 2, "dp")
        for axis in (0, 1):
            if e:
                (gx, gt)[axis][7 - offset(e)].wait_recv()
            for way in (0, 1):
                ring_send(axis, way, 1, e // 2, e % 2)
    for axis in (0, 1):
        for k in (1, 2, 3, 4):
            ends.append(whole(
                S["xg"].at[pl.ds(0, 2)] if k < 4 else S["xg"].at[0],
                S["ring_s"].at[axis, k - 1], S["ring_r"].at[axis, 0, 0, 0]).wait_send)
    lax.fori_loop(0, 4, functools.partial(ring_rest, 2), 0)
    yield "ring2"
    arrive(stb)
    S["stc"][z] = jnp.sum(S["stb"][...], axis=0)
    stc = spread("stc", z, 3, "z")
    lax.fori_loop(0, 4, functools.partial(ring_rest, 3), 0)
    lax.fori_loop(0, 2, ring_last, 0)
    arrive(ggain)
    for load in loads:
        load()
        ends.remove(load)
    total = jnp.zeros((8, H), f32)
    for i in range(8):
        rows = S["gg"][i]
        S["gb"][i] = turned(rows[0:1])[:F]
        total += jnp.dot(rows[:, :F].astype(bf16), S["w1"][F * i:F * (i + 1)], preferred_element_type=f32)
    S["u"][...] = total
    arrive(stc)
    for way in (0, 1):
        ring_wait(0, way, 3, 1 - way)
        ring_wait(0, way, 4, way)
    yield "ringhalf"

    place = [(z + offset(e)) % 8 for e in range(8)]

    def scale_of(tile):
        mean = tile[0:1] / D
        return mean, lax.rsqrt(tile[1:2] / D - mean * mean + epsilon)

    def normed(h):
        for e in range(4 * h, 4 * h + 4):
            mean, inv = scale_of(S["stc"][place[e]])

            def rows(i, carry):
                S["nt"][e, i] = ((S["xg"][place[e], i].astype(f32) - mean) * inv * S["gb"][i]).astype(bf16)
                return carry

            lax.fori_loop(0, 8, rows, 0)

    def joined(ref, spots):
        return jnp.concatenate([ref[i].reshape(K, 128) for i in spots], axis=1)

    def products(h):
        for i in (2 * h, 2 * h + 1):
            lanes = slice(256 * (i % 2), 256 * (i % 2 + 1))
            pre_part = lax.dot_general(
                S["w1"][...], joined(S["nt"], (2 * i, 2 * i + 1)), (((0,), (0,)), ((), ())), preferred_element_type=f32)
            act_part = jnp.dot(S["w2"][...], joined(S["tg"], place[2 * i:2 * i + 2]), preferred_element_type=f32)
            S["part"][h, 0, :, :, :, lanes] = pre_part.reshape(4, 2, Q, 256)
            S["part"][h, 1, :, :, :, lanes] = act_part.reshape(4, 2, Q, 256)
        pairs = {}
        for i in (1, 2, 3, 0):
            to = (chip + i) % 4
            for arr in range(2):
                S["cs"][h, to, arr] = S["part"][h, arr, to, 1 - core].astype(bf16)
            pairs[i] = go(S["cs"].at[h, to], S["cr"].at[h, to], "core", (h, i), at(2 * chip + 1 - core, z, y))
        return pairs

    def chip_sum(h, pairs):
        hops = []
        for i in (1, 2, 3):
            to = (chip + i) % 4
            pairs[i].wait_recv()
            for arr in range(2):
                S["xs"][h, i - 1, arr] = (
                    S["part"][h, arr, to, core] + S["cr"][h, to, arr].astype(f32)).astype(bf16)
            hops.append(go(S["xs"].at[h, i - 1], S["xr"].at[h, i - 1], "xx", (h, i - 1), at(2 * to + core, z, y)))
        return hops

    def activate(h, pairs, hops):
        pairs[0].wait_recv()
        arrive(hops)
        pre_act, act_grad = (
            S["part"][h, arr, chip, core] + S["cr"][h, chip, arr].astype(f32)
            + sum(S["xr"][h, i, arr].astype(f32) for i in range(3)) for arr in range(2))
        value, slope = gelu_parts(pre_act)
        pre_grad = (act_grad * slope).astype(bf16)
        S["comb"][h, d, 0] = value.astype(bf16)
        S["comb"][h, d, 1] = pre_grad
        hops = {
            i: go(S["comb"].at[h, d], S["comb"].at[h, d], "ax", (h, i - 1), at(2 * ((chip + i) % 4) + core, z, y))
            for i in (1, 2, 3)}
        second = jnp.sum(pre_grad.astype(f32) * pre_act, axis=0, keepdims=True)
        for i in range(4):
            S["s2p"][place[4 * h + i]] = jnp.zeros((8, 128), f32)
            S["s2p"][place[4 * h + i], 1:2] = second[:, 128 * i:128 * (i + 1)]
        return hops

    def pass_on(h, hops):
        pairs = []
        for i in (0, 3, 1, 2):
            slot = 2 * ((chip - i + 4) % 4) + core
            if i:
                hops[i].wait_recv()
            ref = S["comb"].at[h, slot]
            pairs.append(go(ref, ref, "ac", (h, i), at(2 * chip + 1 - core, z, y)))
        return pairs

    both = (0, 1)
    normed(0)
    pairs = {0: products(0)}
    hops = {0: chip_sum(0, pairs[0])}
    for way in both:
        ring_wait(0, way, 3, 3 - way)
        ring_wait(0, way, 4, 2 + way)
        for j in both:
            ring_wait(1, way, 3, 2 * j + 1 - way)
            ring_wait(1, way, 4, 2 * j + way)
    normed(1)
    pairs[1] = products(1)
    hops[1] = chip_sum(1, pairs[1])
    yield "chipsum"
    hops = [activate(h, pairs[h], hops[h]) for h in both]
    yield "dpsum"
    pairs = [pass_on(h, hops[h]) for h in both]

    def norm_products(h):
        arrive(pairs[h])
        for i in (2 * h, 2 * h + 1):
            lanes = slice(256 * (i % 2), 256 * (i % 2 + 1))
            out = jnp.dot(
                S["w1"][...], S["comb"][h, :, 1, :, lanes].reshape(H, 256), preferred_element_type=f32)
            S["ng"][2 * i] = out[:, :128].reshape(8, F, 128)
            S["ng"][2 * i + 1] = out[:, 128:].reshape(8, F, 128)

    rs = {}

    def rs_block(axis, dest, h):
        return S["ng"][pl.ds(4 * h, 4), dest, HALF * axis:HALF * (axis + 1)]

    def rs_add(axis, way, k, h, val):
        if (axis, way, k, h) in rs:
            rs[axis, way, k, h].wait_recv()
            val = val + S["ra"][axis, k - 1, way, pl.ds(4 * h, 4)].astype(f32)
        return val

    def rs_round(r, h):
        for axis in both:
            for way in both:
                k = r + 1 if h == way else r + 2
                if k > 4:
                    continue
                sign = 1 - 2 * way
                val = rs_block(axis, (y + sign * (5 - k) + 8) % 8, h)
                val = rs_add(axis, way, k - 1, h, val)
                half = pl.ds(4 * h, 4)
                S["sa"][axis, k - 1, way, half] = val.astype(bf16)
                rs[axis, way, k, h] = pltpu.make_async_remote_copy(
                    src_ref=S["sa"].at[axis, k - 1, way, half], dst_ref=S["ra"].at[axis, k - 1, way, half],
                    send_sem=S["rs_s"].at[axis, k - 1], recv_sem=S["rs_r"].at[axis, way, k - 1, h],
                    device_id=along("y", sign + 8), device_id_type=MESH)
                rs[axis, way, k, h].start()

    yield "passon"
    norm_products(0)
    rs_round(0, 0)
    norm_products(1)
    yield "dpgather"
    rs_round(0, 1)
    def hidden(arr):
        return jnp.concatenate([S["comb"][h, :, arr].reshape(H, 512) for h in both], axis=1)

    pg = hidden(1)
    high = S["u"][...].astype(bf16)
    low = (S["u"][...] - high.astype(f32)).astype(bf16)
    first = jnp.dot(high, pg, preferred_element_type=f32) + jnp.dot(low, pg, preferred_element_type=f32)
    for i in range(8):
        S["s2p"][place[i], 0:1] = first[0:1, 128 * i:128 * (i + 1)]
    s2a = spread("s2r", d, 4, "dp", lambda i: S["s2p"].at[(d + i) % 8])
    S["s2r"][d] = S["s2p"][d]
    rs_round(1, 0)
    rs_round(1, 1)
    arrive(s2a)
    S["s2y"][y] = jnp.sum(S["s2r"][...], axis=0)
    rs_round(2, 0)
    rs_round(2, 1)
    s2b = spread("s2y", y, 5, "y")
    rs_round(3, 0)
    rs_round(3, 1)
    for axis in both:
        for k in (1, 2, 3, 4):
            ends.append(whole(
                S["sa"].at[axis, k - 1, 0] if k == 1 else S["sa"].at[axis, k - 1],
                S["rs_s"].at[axis, k - 1], S["rs_r"].at[axis, 0, 0, 0]).wait_send)

    def parts(axis):
        for h in both:
            val = rs_block(axis, y, h)
            for way in both:
                val = rs_add(axis, way, 4, h, val)
            for i in range(4):
                S["ng"][4 * h + i, y, HALF * axis:HALF * (axis + 1)] = val[i]
                S["fs"][axis, place[4 * h + i]] = val[i].astype(bf16)
        S["ft"][axis, d] = S["fs"][axis, d]
        return scatter(S["ft"].at[axis], d, 7 + axis, "dp", lambda i: S["fs"].at[axis, (d + i) % 8])

    def to_owners(axis):
        S["fr"][axis, z] = S["ft"][axis, z]
        return scatter(S["fr"].at[axis], z, 9 + axis, "z", lambda i: S["ft"].at[axis, (z + i) % 8])

    blocks = [parts(axis) for axis in both]
    yield "rings"
    total = jnp.zeros((F, 128), f32)
    for i in range(8):
        mean, inv = scale_of(S["stc"][place[i]])
        total += S["ng"][i, y] * ((S["xg"][place[i], y].astype(f32) - mean) * inv)
    S["pad"][:F] = total
    S["gs"][d] = jnp.broadcast_to(jnp.sum(S["pad"][...].T, axis=0, keepdims=True), (8, 128))
    gains = spread("gs", d, 11, "dp")
    arrive(s2b)
    S["s2z"][z] = jnp.sum(S["s2y"][...], axis=0)
    s2c = spread("s2z", z, 6, "z")
    arrive(blocks[0])
    owned = [to_owners(0)]
    arrive(blocks[1])
    owned.append(to_owners(1))
    arrive(gains)
    S["gr"][z] = S["gs"][z]
    gain_parts = spread("gr", z, 12, "z", lambda i: S["gs"].at[(z + i) % 8])
    nt_all = joined(S["nt"], range(8))
    S["w1g"][...] = lax.dot_general(nt_all, hidden(1), (((1,), (1,)), ((), ())), preferred_element_type=f32)
    ends.append(local(S["w1g"], w1g_hbm, 5).wait)
    tg_all = joined(S["tg"], place)
    S["w2g"][...] = lax.dot_general(hidden(0), tg_all, (((1,), (1,)), ((), ())), preferred_element_type=f32)
    ends.append(local(S["w2g"], w2g_hbm, 6).wait)
    gcol = turned(S["gown"][0:1])[:F]
    mean, inv = scale_of(S["stc"][d])
    cen = (S["xo"][...].astype(f32) - mean) * inv
    arrive(s2c)
    tile = jnp.sum(S["s2z"][...], axis=0)
    base = S["to"][...].astype(f32) - inv * (tile[0:1] / D + cen * (tile[1:2] / D))
    for axis in both:
        arrive(owned[axis])
    grad = jnp.concatenate([jnp.sum(S["fr"][axis].astype(f32), axis=0) for axis in both], axis=0)
    S["igv"][...] = (base + inv * (grad * gcol)).astype(bf16)
    ends.append(local(S["igv"], ig_hbm, 7).wait)
    arrive(gain_parts)
    S["ggv"][...] = jnp.sum(S["gr"][...], axis=0)[0:1, :F]
    ends.append(local(S["ggv"], gg_hbm, 8).wait)


def hand_over(*refs):
    ins, outs, held, sem = refs[:4], refs[4:8], refs[8:12], refs[12]
    steps = []
    for i in (2, 3, 0, 1):
        rows = ins[i].shape[0] // 4
        for part in range(4 if i < 2 else 1):
            span = pl.ds(rows * part, rows) if i < 2 else slice(None)
            steps.append((
                pltpu.make_async_copy(ins[i].at[span], held[i].at[span], sem.at[0, i, part]),
                pltpu.make_async_copy(held[i].at[span], outs[i].at[span], sem.at[1, i, part])))
    for load, _ in steps:
        load.start()
    for load, store in steps:
        load.wait()
        store.start()
    for _, store in steps:
        store.wait()


def shards(inputs, gain, w_in, w_out, targets):
    hbm = pl.BlockSpec(memory_space=pl.ANY)
    scratch = [pltpu.VMEM(shape, kind) for shape, kind in SCRATCH.values()]
    scratch += [pltpu.SemaphoreType.DMA(shape) for shape in SEMS.values()]
    results = (
        jax.ShapeDtypeStruct((K, H), f32), jax.ShapeDtypeStruct((H, K), f32),
        jax.ShapeDtypeStruct((F, 128), bf16), jax.ShapeDtypeStruct((1, F), f32))
    input_grad, gain_grad, w_in_grad, w_out_grad = pl.pallas_call(
        kernel,
        out_shape=(*results[2:], *results[:2]),
        in_specs=[hbm] * 5,
        out_specs=(hbm,) * 4,
        scratch_shapes=scratch,
        compiler_params=pltpu.CompilerParams(
            collective_id=0, has_side_effects=True, vmem_limit_bytes=60 * 1024 * 1024),
        cost_estimate=pl.CostEstimate(flops=2 * 10 ** 9, bytes_accessed=4 * 10 ** 6, transcendentals=10 ** 5),
        name="backward",
    )(inputs.T, targets.T, gain.reshape(1, F), w_in, w_out)
    w_in_grad, w_out_grad, input_grad, gain_grad = pl.pallas_call(
        hand_over,
        out_shape=results,
        in_specs=[hbm] * 4,
        out_specs=(hbm,) * 4,
        scratch_shapes=[pltpu.VMEM(out.shape, out.dtype) for out in results] + [pltpu.SemaphoreType.DMA((2, 4, 4))],
        compiler_params=pltpu.CompilerParams(vmem_limit_bytes=60 * 1024 * 1024),
        cost_estimate=pl.CostEstimate(flops=0, bytes_accessed=3 * 10 ** 6, transcendentals=0),
        name="hand_over",
    )(w_in_grad, w_out_grad, input_grad, gain_grad)
    return input_grad.T, gain_grad.reshape(F), w_in_grad, w_out_grad


def solution(mesh):
    return jax.shard_map(
        shards,
        mesh=mesh,
        in_specs=(P("dp", "mp"), P("mp"), P("dp", "mp"), P("mp", "dp"), P("dp", "mp")),
        out_specs=(P("dp", "mp"), P("mp"), P("dp", "mp"), P("mp", "dp")),
        check_vma=False,
    )
```
